256 devices in a mesh: band: 4 (over x_lo, core), space: 64 (over x_hi, y, z).
Axes of the slice: x: 4 (x_hi: 2, x_lo: 2; x = x_hi * 2 + x_lo), y: 4, z: 8, core: 2. Of those that a mesh axis runs over, the one named last changes fastest.
Arguments:
- orbitals: bfloat16 [96, 1024, 16, 128], P('band', 'space'), may hold values from -0.796875 to 0.796875
- occupations: float32 [96], P('band'), may hold values from 0.5 to 2
- potential_in: float32 [1024, 16, 128], P('space'), may hold values from -6 to 6
- ionic_potential: float32 [1024, 16, 128], P('space'), may hold values from -6 to 6
- hartree_prev: float32 [1024, 16, 128], P('space'), may hold values from -6 to 6
- projectors: bfloat16 [512, 13, 16, 256], P('space'), may hold values from -0.375 to 0.375
- box_start: int32 [3, 512], replicated, may hold values from 0 to 1023, as said below
- coupling: float32 [13, 13], replicated, may hold values from -6 to 6
Outputs:
- applied: bfloat16 [96, 1024, 16, 128], P('band', 'space')
- potential: float32 [1024, 16, 128], P('space')
The draws below stay inside these ranges and needn't reach their ends.
Inputs may be any that keep to these rules, and one draw needn't show every extreme that they name: `box_start`: column a holds the first plane, row and column of atom a's box. The plane lies among the 16 planes that begin at (a // 8) * 16; the row is at most 0 and the column at most 112. Atom 0's box begins at plane, row and column 0, and the last atom's box begins on plane 1024 - 1.
All inputs are finite; a program needn't handle non-finite values.
Results may differ from the reference program's by a relative error of at most 0.013.
Values may be sent and summed in bfloat16 or wider, within the bound.
A program may use at most 128 MiB of HBM per device.

```python
import math
import jax
import jax.numpy as jnp
from jax import lax

NORB = 96
NPROJ = 13
BOX = 16
PLANES = 16
NY = 16
NZ = 128
ATOM_DEV = 8
SWEEPS = 2
NX = 1024
ATOMS = 512


def draw_box_start(key, part):
    key_plane, key_row, key_col = jax.random.split(key, 3)
    atom_index = jnp.arange(ATOMS, dtype=jnp.int32)
    owners = atom_index // ATOM_DEV
    offset = jax.random.randint(key_plane, (ATOMS,), 0, PLANES, dtype=jnp.int32)
    offset = jnp.where(atom_index == 0, 0, jnp.where(atom_index == ATOMS - 1, PLANES - 1, offset))
    row_start = jax.random.randint(key_row, (ATOMS,), 0, NY - BOX + 1, dtype=jnp.int32)
    row_start = jnp.where(atom_index == 0, 0, row_start)
    col_start = jax.random.randint(key_col, (ATOMS,), 0, NZ - BOX + 1, dtype=jnp.int32)
    col_start = jnp.where(atom_index == 0, 0, col_start)
    return jnp.stack([owners * PLANES + offset, row_start, col_start]).astype(jnp.int32)


def levels(rng, extent, cuts, smallest, top_value):
    def one(position, parts):
        heights = jax.random.uniform(jax.random.fold_in(jax.random.fold_in(rng, 6), position), (parts,), jnp.float32, smallest / len(cuts), top_value / len(cuts))
        return jnp.repeat(jnp.exp(heights), extent[position] // parts).reshape((-1,) + (1,) * (len(extent) - position - 1))

    gain = one(*cuts[0])
    for cut in cuts[1:]:
        gain = gain * one(*cut)
    return gain


def centred(stream_key, dims, deviation, reach, cuts=(), kind=jnp.bfloat16):
    loudness = levels(stream_key, dims, cuts, -0.22, 0.18) if cuts else 1.0
    values = jax.random.normal(stream_key, dims, jnp.float32) * deviation * loudness
    return jnp.minimum(jnp.maximum(values, -reach), reach).astype(kind)


def setup_inputs(seed: int = 0) -> dict:
    keys = jax.random.split(jax.random.key(seed), 9)
    return {
        "orbitals": centred(keys[0], (NORB, NX, NY, NZ), 0.1, 0.796875, ((0, 4), (1, 64))),
        "occupations": jnp.clip(0.5 + 1.5 * jax.random.uniform(keys[1], (NORB,), jnp.float32) ** levels(keys[1], (NORB,), ((0, 4),), -0.2, 0.2), 0.5, 2.0),
        "potential_in": centred(keys[2], (NX, NY, NZ), 1.0, 6.0, ((0, 64),), jnp.float32),
        "ionic_potential": centred(keys[3], (NX, NY, NZ), 1.0, 6.0, ((0, 64),), jnp.float32),
        "hartree_prev": centred(keys[4], (NX, NY, NZ), 1.0, 6.0, ((0, 64),), jnp.float32),
        "projectors": centred(keys[5], (ATOMS, NPROJ, BOX, BOX * BOX), (BOX * BOX) ** -0.5, 0.375, ((0, 64),)),
        "box_start": draw_box_start(jax.random.fold_in(keys[8], 71), 0),
        "coupling": centred(keys[7], (NPROJ, NPROJ), 1.0, 6.0, (), jnp.float32),
    }


screening = 0.25
stencil_far = ((1, 4.0 / 3.0), (2, -1.0 / 12.0))


def fourth_order(field):
    summed = -7.5 * field
    for distance, weight in stencil_far:
        for dimension in (0, 1, 2):
            summed = summed + weight * (jnp.roll(field, distance, dimension) + jnp.roll(field, -distance, dimension))
    return summed


def reference(orbitals, occupations, potential_in, ionic_potential, hartree_prev, projectors, box_start, coupling):
    steps_box = jnp.arange(BOX, dtype=jnp.int32)
    plane_index = (box_start[0][:, None] + steps_box[None, :]) % NX
    row_index = box_start[1][:, None] + steps_box[None, :]
    col_index = box_start[2][:, None] + steps_box[None, :]
    linear = (plane_index[:, :, None, None] * NY + row_index[:, None, :, None]) * NZ + col_index[:, None, None, :]
    linear = linear.reshape(ATOMS, BOX, BOX * BOX).astype(jnp.int32)
    flat_index = linear.reshape(-1)
    beta_wide = projectors.astype(jnp.float32)
    coupling_wide = coupling.astype(jnp.float32)

    def per_orbital(density, inputs):
        orbital, weight = inputs
        field = orbital.astype(jnp.float32)
        local_part = -0.5 * fourth_order(field) + potential_in * field
        boxes = orbital.reshape(-1)[linear].astype(jnp.float32)
        coefficients = jnp.einsum("apxk,axk->ap", beta_wide, boxes)
        weighted = jnp.dot(coefficients, coupling_wide.T, precision=lax.Precision.HIGHEST).astype(jnp.bfloat16)
        weighted = lax.optimization_barrier(weighted).astype(jnp.float32)
        contrib = jnp.einsum("apxk,ap->axk", beta_wide, weighted)
        nonlocal_part = jnp.zeros((NX * NY * NZ,), jnp.float32).at[flat_index].add(contrib.reshape(-1))
        applied_one = (local_part + nonlocal_part.reshape(NX, NY, NZ)).astype(jnp.bfloat16)
        density = density + weight * field * field
        return density, applied_one

    density, applied = lax.scan(per_orbital, jnp.zeros((NX, NY, NZ), jnp.float32), (orbitals, occupations.astype(jnp.float32)))
    mean_density = jnp.mean(density)
    source = 4.0 * math.pi * (density - mean_density)
    hartree = hartree_prev
    for sweep_index in range(SWEEPS):
        neighbours = jnp.zeros_like(hartree)
        for dimension in (0, 1, 2):
            neighbours = neighbours + jnp.roll(hartree, 1, dimension) + jnp.roll(hartree, -1, dimension)
        hartree = (neighbours + source) / (6.0 + screening)
    potential = ionic_potential + hartree - jnp.cbrt(3.0 * density / math.pi)
    return applied, potential
```

```python
import functools
import math

import jax
import jax.numpy as jnp
import numpy as np
from jax import lax
from jax.experimental import pallas as pl
from jax.experimental.pallas import tpu as pltpu
from jax.sharding import PartitionSpec as P

SCREENING = 0.25
SWEEPS = 2
FOUR_PI = 4.0 * math.pi
ROWGROUP = 8
MESH = pl.DeviceIdType.MESH
F32 = jnp.float32
BF16 = jnp.bfloat16
SLOT = 16


def stencil_matrices(planes, rows, cols):
    def line(count, periodic):
        matrix = np.zeros((count, count), np.float32)
        for distance, weight in ((1, 16.0), (2, -1.0)):
            for sign in (-1, 1):
                for index in range(count):
                    other = index + sign * distance
                    if periodic:
                        other %= count
                    if 0 <= other < count:
                        matrix[index, other] += weight
        return matrix

    left = np.kron(line(planes, False), np.eye(rows)) + np.kron(np.eye(planes), line(rows, True))
    right = line(cols, True) - 90.0 * np.eye(cols)
    return left.astype(np.float32), right.astype(np.float32)


def kernel(
    dims,
    box_ref,
    occ_ref,
    coup_ref,
    orb_ref,
    vin_ref,
    ion_ref,
    har_ref,
    proj_ref,
    left_ref,
    right_ref,
    app_ref,
    pot_ref,
    pprev,
    halo,
    hhalo,
    rhalo,
    dens_f,
    dens_b,
    dens_in,
    rho,
    chg1,
    chg2,
    chg3,
    chg_in1,
    chg_in2,
    chg_in3,
    colmat,
    scat,
    local_part,
    gathered,
    mask3,
    shifts,
    spread,
    packed,
    part_own,
    part_prev,
    got_own,
    got_prev,
    couple,
    nlt,
    hone,
    s_proj,
    r_proj,
    s_fwd,
    r_fwd,
    s_halo,
    r_halo,
    s_hh,
    r_hh,
    s_dens,
    r_dens,
    s_c1,
    r_c1,
    s_c2,
    r_c2,
    s_c3,
    r_c3,
    s_rh,
    r_rh,
    s_part,
    r_part,
):
    n_band, n_space, group = dims
    orbs, planes, rows, cols = orb_ref.shape
    atoms, nproj, width, square = proj_ref.shape
    cells = planes * rows
    n_far = n_space // group
    half = atoms // 2
    quarter = half // 2

    me_b = lax.axis_index("band")
    me_s = lax.axis_index("space")
    nxt = lax.rem(me_s + 1, n_space)
    prv = lax.rem(me_s + n_space - 1, n_space)
    core = lax.rem(me_b, 2)
    sib = me_b + 1 - 2 * core
    near = lax.rem(me_s, group)
    far = me_s // group

    def band_peer(d):
        return (lax.rem(me_b + d, n_band), me_s)

    def near_peer(d):
        return (me_b, far * group + lax.rem(near + d, group))

    def far_peer(d):
        return (me_b, lax.rem(far + d, n_far) * group + near)

    partners = [(me_b, nxt), (me_b, prv)]
    partners += [band_peer(d) for d in range(1, n_band)]
    partners += [near_peer(d) for d in range(1, group)]
    partners += [far_peer(d) for d in range(1, n_far)]
    barrier = pltpu.get_barrier_semaphore()
    for partner in partners:
        pl.semaphore_signal(barrier, inc=1, device_id=partner, device_id_type=MESH)
    pl.semaphore_wait(barrier, len(partners))

    sent = []

    def send(src, dst, send_sem, recv_sem, device):
        copy = pltpu.make_async_remote_copy(
            src_ref=src,
            dst_ref=dst,
            send_sem=send_sem,
            recv_sem=recv_sem,
            device_id=device,
            device_id_type=MESH,
        )
        copy.start()
        sent.append(copy)

    def arrived(dst, send_sem, recv_sem):
        pltpu.make_async_remote_copy(
            src_ref=dst,
            dst_ref=dst,
            send_sem=send_sem,
            recv_sem=recv_sem,
            device_id=(me_b, nxt),
            device_id_type=MESH,
        ).wait_recv()

    for h in range(2):
        some = pl.ds(core * half + h * quarter, quarter)
        send(proj_ref.at[some], pprev.at[some], s_proj.at[h], r_proj.at[h], (me_b, nxt))
    send(orb_ref.at[:, pl.ds(0, 2)], halo.at[1], s_halo.at[1], r_halo.at[1], (me_b, prv))
    send(har_ref.at[pl.ds(0, 2)], hhalo.at[1], s_hh.at[1], r_hh.at[1], (me_b, prv))
    send(har_ref.at[pl.ds(planes - 2, 2)], hhalo.at[0], s_hh.at[0], r_hh.at[0], (me_b, nxt))
    send(orb_ref.at[:, pl.ds(planes - 2, 2)], halo.at[0], s_halo.at[0], r_halo.at[0], (me_b, nxt))

    def density_plane(i, charge):
        total = jnp.zeros((rows, cols), F32)
        for o in range(orbs):
            field = orb_ref[o, i].astype(F32)
            total = total + (occ_ref[o] * field) * field
        dens_f[i] = total
        dens_b[i] = total.astype(BF16)
        for r in range(0, rows, ROWGROUP):
            charge = charge + total[r : r + ROWGROUP]
        return charge

    chg1[...] = lax.fori_loop(0, planes, density_plane, jnp.zeros((ROWGROUP, cols), F32))
    for d in range(1, n_band):
        send(dens_b, dens_in.at[me_b], s_dens.at[d], r_dens.at[me_b], band_peer(d))
        send(chg1, chg_in1.at[me_b], s_c1.at[d], r_c1.at[me_b], band_peer(d))

    def lane_table(first, which):
        lane = lax.broadcasted_iota(jnp.int32, (1, cols), 1)
        table = lax.rem(lane, SLOT)
        for a in range(atoms):
            table = table + jnp.where(lane // SLOT == a, box_ref[which, first + a], 0)
        return table

    first_own = me_s * atoms
    first_prev = prv * atoms
    colmat[:, 0:cols] = right_ref[...]
    zrow = lax.broadcasted_iota(jnp.int32, (cols, cols), 0)
    for part, first in ((0, first_own), (1, first_prev)):
        hot = jnp.where(zrow == lane_table(first, 2), 1.0, 0.0).astype(F32)
        colmat[:, (1 + part) * cols : (2 + part) * cols] = hot.astype(BF16)
        scat[part * cols : (part + 1) * cols, :] = hot.T.astype(BF16)

    def stencil(o, carry):
        field = orb_ref[o].reshape(cells, cols)
        summed = jnp.dot(left_ref[...], field, preferred_element_type=F32)
        wide = jnp.dot(field, colmat[...], preferred_element_type=F32)
        lap = summed + wide[:, 0:cols]
        local_part[o] = lap * (-0.5 / 12.0) + vin_ref[...].reshape(cells, cols) * field.astype(F32)
        gathered[0, pl.ds(o, cells, stride=orbs), :] = wide[:, cols : 2 * cols]
        gathered[1, pl.ds(o, cells, stride=orbs), :] = wide[:, 2 * cols : 3 * cols]
        return carry

    lax.fori_loop(0, orbs, stencil, 0)

    for d in range(1, n_band):
        peer = lax.rem(me_b + d, n_band)
        arrived(chg_in1.at[peer], s_c1.at[d], r_c1.at[peer])
    charge = chg1[...]
    for d in range(1, n_band):
        charge = charge + chg_in1[lax.rem(me_b + d, n_band)]
    chg2[...] = charge
    for d in range(1, group):
        send(chg2, chg_in2.at[near], s_c2.at[d], r_c2.at[near], near_peer(d))
    for d in range(1, n_band):
        peer = lax.rem(me_b + d, n_band)
        arrived(dens_in.at[peer], s_dens.at[d], r_dens.at[peer])
    total_density = dens_f[...]
    for d in range(1, n_band):
        total_density = total_density + dens_in[lax.rem(me_b + d, n_band)].astype(F32)
    rho[...] = total_density
    send(rho.at[0], rhalo.at[1], s_rh.at[1], r_rh.at[1], (me_b, prv))
    send(rho.at[planes - 1], rhalo.at[0], s_rh.at[0], r_rh.at[0], (me_b, nxt))

    spot = lax.broadcasted_iota(jnp.int32, (atoms, SLOT, cols), 2) // SLOT
    mask3[...] = jnp.where(
        spot == lax.broadcasted_iota(jnp.int32, (atoms, SLOT, cols), 0), 1.0, 0.0
    ).astype(BF16)
    r_idx = lax.broadcasted_iota(jnp.int32, (cells, nproj * width), 0)
    c_idx = lax.broadcasted_iota(jnp.int32, (cells, nproj * width), 1)
    shifts[...] = jnp.where(
        r_idx % SLOT == c_idx // width, r_idx // SLOT - c_idx % width, 4 * planes
    )

    def pack(part, source, first):
        for a in range(atoms):
            plane = lax.rem(box_ref[0, first + a], planes) - part * planes
            place = jnp.where(shifts[...] == plane, 1.0, 0.0).astype(BF16)
            spread[a] = jnp.dot(
                place, source[a].reshape(nproj * width, square), preferred_element_type=F32
            )

        slot = lax.broadcasted_iota(jnp.int32, (SLOT, cols), 1) // SLOT

        def turn(i, carry):
            at = pl.ds(pl.multiple_of(i * SLOT, SLOT), SLOT)
            for h in range(square // cols):
                x = [spread[a, at, h * cols : (h + 1) * cols] for a in range(atoms)]
                for d in (4, 2, 1):
                    low = (slot & d) == 0
                    for a in range(atoms):
                        if a & d:
                            continue
                        lo, hi = x[a], x[a + d]
                        x[a] = jnp.where(low, lo, pltpu.roll(hi, d * SLOT, 1))
                        x[a + d] = jnp.where(low, pltpu.roll(lo, cols - d * SLOT, 1), hi)
                for y in range(atoms):
                    packed[part, h * atoms + y, i] = x[y].astype(BF16)
            return carry

        lax.fori_loop(0, planes, turn, 0)

    def block(part, y, i):
        tile = packed[part, y, i]
        return (tile[None] * mask3[...]).reshape(atoms * SLOT, cols)

    def gather(part):
        def one(i, total):
            for y in range(0, rows, 2):
                base = pl.multiple_of((i * rows + y) * orbs, 8)
                boxes = jnp.concatenate(
                    [
                        gathered[part, pl.ds(base, orbs), :],
                        gathered[part, pl.ds(base + orbs, orbs), :],
                    ],
                    axis=1,
                ).astype(BF16)
                weights = jnp.concatenate([block(part, y, i), block(part, y + 1, i)], axis=1)
                total = total + lax.dot_general(
                    boxes, weights, (((1,), (1,)), ((), ())), preferred_element_type=F32
                )
            return total

        return lax.fori_loop(0, planes, one, jnp.zeros((orbs, atoms * SLOT), F32))

    pack(0, proj_ref, first_own)
    part_own[...] = gather(0)
    send(part_own, got_prev, s_part.at[0], r_part.at[0], (me_b, nxt))

    for d in range(1, group):
        peer = lax.rem(near + d, group)
        arrived(chg_in2.at[peer], s_c2.at[d], r_c2.at[peer])
    charge = chg2[...]
    for d in range(1, group):
        charge = charge + chg_in2[lax.rem(near + d, group)]
    chg3[...] = charge
    for d in range(1, n_far):
        send(chg3, chg_in3.at[far], s_c3.at[d], r_c3.at[far], far_peer(d))

    for h in range(2):
        some = pl.ds(core * half + h * quarter, quarter)
        arrived(pprev.at[some], s_proj.at[h], r_proj.at[h])
        send(pprev.at[some], pprev.at[some], s_fwd.at[h], r_fwd.at[h], (sib, me_s))
    for h in range(2):
        some = pl.ds((1 - core) * half + h * quarter, quarter)
        arrived(pprev.at[some], s_fwd.at[h], r_fwd.at[h])
    pack(1, pprev, first_prev)
    part_prev[...] = gather(1)
    send(part_prev, got_own, s_part.at[1], r_part.at[1], (me_b, prv))

    for side in range(2):
        arrived(hhalo.at[side], s_hh.at[side], r_hh.at[side])
        arrived(rhalo.at[side], s_rh.at[side], r_rh.at[side])

    def around(cell):
        return (
            pltpu.roll(cell, 1, 0)
            + pltpu.roll(cell, rows - 1, 0)
            + pltpu.roll(cell, 1, 1)
            + pltpu.roll(cell, cols - 1, 1)
        )

    def start_plane(p):
        if p < 0:
            return hhalo[0, p + 2]
        if p >= planes:
            return hhalo[1, p - planes]
        return har_ref[p]

    def rho_plane(p):
        if p < 0:
            return rhalo[0]
        if p >= planes:
            return rhalo[1]
        return rho[p]

    inverse = 1.0 / (6.0 + SCREENING)
    for p in range(-1, planes + 1):
        total = start_plane(p - 1) + start_plane(p + 1) + around(start_plane(p))
        hone[p + 1] = (total + FOUR_PI * rho_plane(p)) * inverse
    for d in range(1, n_far):
        peer = lax.rem(far + d, n_far)
        arrived(chg_in3.at[peer], s_c3.at[d], r_c3.at[peer])
    charge = chg3[...]
    for d in range(1, n_far):
        charge = charge + chg_in3[lax.rem(far + d, n_far)]
    mean = jnp.sum(charge, axis=(0, 1), keepdims=True) * (1.0 / (cells * cols * n_space))
    lift = FOUR_PI * inverse * (1.0 + 6.0 * inverse) * mean
    for p in range(planes):
        total = hone[p] + hone[p + 2] + around(hone[p + 1])
        second = (total + FOUR_PI * rho[p]) * inverse
        root = jnp.exp(jnp.log(rho[p] * (3.0 / math.pi)) * (1.0 / 3.0))
        pot_ref[p] = ion_ref[p] + (second - lift) - root

    for side in range(2):
        arrived(halo.at[side], s_halo.at[side], r_halo.at[side])

    def edges(o, carry):
        near_low, far_low = halo[0, o, 1].astype(F32), halo[0, o, 0].astype(F32)
        near_up, far_up = halo[1, o, 0].astype(F32), halo[1, o, 1].astype(F32)
        scale = -0.5 / 12.0
        last = cells - rows
        local_part[o, 0:rows] += scale * (16.0 * near_low - far_low)
        local_part[o, rows : 2 * rows] += (-scale) * near_low
        local_part[o, last : last + rows] += scale * (16.0 * near_up - far_up)
        local_part[o, last - rows : last] += (-scale) * near_up
        return carry

    lax.fori_loop(0, orbs, edges, 0)

    row_id = lax.broadcasted_iota(jnp.int32, (atoms * SLOT, nproj), 0) % SLOT
    pick = jnp.where(
        row_id == lax.broadcasted_iota(jnp.int32, (atoms * SLOT, nproj), 1), 1.0, 0.0
    ).astype(F32)
    contract = (((1,), (1,)), ((), ()))
    tall = lax.dot_general(
        pick, coup_ref[...], contract, precision=lax.Precision.HIGHEST, preferred_element_type=F32
    )
    full = lax.dot_general(
        tall, pick, contract, precision=lax.Precision.HIGHEST, preferred_element_type=F32
    )
    size = (atoms * SLOT, atoms * SLOT)
    same = (
        lax.broadcasted_iota(jnp.int32, size, 0) // SLOT
        == lax.broadcasted_iota(jnp.int32, size, 1) // SLOT
    )
    couple[...] = jnp.where(same, full, 0.0)

    arrived(got_prev, s_part.at[0], r_part.at[0])
    arrived(got_own, s_part.at[1], r_part.at[1])
    weighted = []
    for mine, other in ((part_own, got_own), (part_prev, got_prev)):
        weighted.append(
            jnp.dot(
                mine[...] + other[...],
                couple[...],
                precision=lax.Precision.HIGHEST,
                preferred_element_type=F32,
            ).astype(BF16)
        )

    def deposit(i, carry):
        spreads = []
        for part in range(2):
            terms = [
                jnp.dot(weighted[part], block(part, y, i), preferred_element_type=F32)
                for y in range(rows)
            ]
            spreads.append(jnp.concatenate(terms, axis=0).astype(BF16))
        nlt[...] = jnp.dot(
            jnp.concatenate(spreads, axis=1), scat[...], preferred_element_type=F32
        )
        at = pl.ds(pl.multiple_of(i * rows, rows), rows)
        for o in range(orbs):
            total = local_part[o, at, :] + nlt[pl.ds(o, rows, stride=orbs), :]
            app_ref[o, i] = total.astype(BF16)
        return carry

    lax.fori_loop(0, planes, deposit, 0)

    for copy in sent:
        copy.wait_send()


def local(
    n_band,
    n_space,
    orbitals,
    occupations,
    potential_in,
    ionic_potential,
    hartree_prev,
    projectors,
    box_start,
    coupling,
):
    orbs, planes, rows, cols = orbitals.shape
    atoms, nproj, width, square = projectors.shape
    cells = planes * rows
    group = 8 if n_space % 8 == 0 else 2
    n_far = n_space // group
    left, right = stencil_matrices(planes, rows, cols)
    packed_rows = atoms * SLOT
    vmem = pl.BlockSpec(memory_space=pltpu.VMEM)
    smem = pl.BlockSpec(memory_space=pltpu.SMEM)
    dma = pltpu.SemaphoreType.DMA
    scratch = [
        pltpu.VMEM(projectors.shape, BF16),
        pltpu.VMEM((2, orbs, 2, rows, cols), BF16),
        pltpu.VMEM((2, 2, rows, cols), F32),
        pltpu.VMEM((2, rows, cols), F32),
        pltpu.VMEM((planes, rows, cols), F32),
        pltpu.VMEM((planes, rows, cols), BF16),
        pltpu.VMEM((n_band, planes, rows, cols), BF16),
        pltpu.VMEM((planes, rows, cols), F32),
        pltpu.VMEM((ROWGROUP, cols), F32),
        pltpu.VMEM((ROWGROUP, cols), F32),
        pltpu.VMEM((ROWGROUP, cols), F32),
        pltpu.VMEM((n_band, ROWGROUP, cols), F32),
        pltpu.VMEM((group, ROWGROUP, cols), F32),
        pltpu.VMEM((n_far, ROWGROUP, cols), F32),
        pltpu.VMEM((cols, 3 * cols), BF16),
        pltpu.VMEM((2 * cols, cols), BF16),
        pltpu.VMEM((orbs, cells, cols), F32),
        pltpu.VMEM((2, cells * orbs, cols), F32),
        pltpu.VMEM((atoms, SLOT, cols), BF16),
        pltpu.VMEM((cells, nproj * width), jnp.int32),
        pltpu.VMEM((atoms, cells, square), F32),
        pltpu.VMEM((2, rows, planes, SLOT, cols), BF16),
        pltpu.VMEM((orbs, packed_rows), F32),
        pltpu.VMEM((orbs, packed_rows), F32),
        pltpu.VMEM((orbs, packed_rows), F32),
        pltpu.VMEM((orbs, packed_rows), F32),
        pltpu.VMEM((packed_rows, packed_rows), F32),
        pltpu.VMEM((rows * orbs, cols), F32),
        pltpu.VMEM((planes + 2, rows, cols), F32),
        dma((2,)),
        dma((2,)),
        dma((2,)),
        dma((2,)),
        dma((2,)),
        dma((2,)),
        dma((2,)),
        dma((2,)),
        dma((n_band,)),
        dma((n_band,)),
        dma((n_band,)),
        dma((n_band,)),
        dma((group,)),
        dma((group,)),
        dma((n_far,)),
        dma((n_far,)),
        dma((2,)),
        dma((2,)),
        dma((2,)),
        dma((2,)),
    ]
    return pl.pallas_call(
        functools.partial(kernel, (n_band, n_space, group)),
        out_shape=(
            jax.ShapeDtypeStruct(orbitals.shape, BF16),
            jax.ShapeDtypeStruct(potential_in.shape, F32),
        ),
        in_specs=[smem, smem] + [vmem] * 8,
        out_specs=(vmem, vmem),
        scratch_shapes=scratch,
        compiler_params=pltpu.CompilerParams(
            collective_id=0, has_side_effects=True, vmem_limit_bytes=56 * 1024 * 1024
        ),
    )(
        box_start,
        occupations,
        coupling,
        orbitals,
        potential_in,
        ionic_potential,
        hartree_prev,
        projectors,
        jnp.asarray(left, BF16),
        jnp.asarray(right, BF16),
    )


def solution(mesh):
    return jax.shard_map(
        functools.partial(local, mesh.shape["band"], mesh.shape["space"]),
        mesh=mesh,
        in_specs=(
            P("band", "space", None, None),
            P("band"),
            P("space", None, None),
            P("space", None, None),
            P("space", None, None),
            P("space", None, None, None),
            P(),
            P(),
        ),
        out_specs=(P("band", "space", None, None), P("space", None, None)),
        check_vma=False,
    )
```

```python
import functools
import math

import jax
import jax.numpy as jnp
import numpy as np
from jax import lax
from jax.experimental import pallas as pl
from jax.experimental.pallas import tpu as pltpu
from jax.sharding import PartitionSpec as P

SCREENING = 0.25
SWEEPS = 2
FOUR_PI = 4.0 * math.pi
ROWGROUP = 8
MESH = pl.DeviceIdType.MESH
F32 = jnp.float32
BF16 = jnp.bfloat16
SLOT = 16


def stencil_matrices(planes, rows, cols):
    def line(count, periodic):
        matrix = np.zeros((count, count), np.float32)
        for distance, weight in ((1, 16.0), (2, -1.0)):
            for sign in (-1, 1):
                for index in range(count):
                    other = index + sign * distance
                    if periodic:
                        other %= count
                    if 0 <= other < count:
                        matrix[index, other] += weight
        return matrix

    left = np.kron(line(planes, False), np.eye(rows)) + np.kron(np.eye(planes), line(rows, True))
    right = np.kron(np.eye(2), line(cols, True) - 90.0 * np.eye(cols))
    return left.astype(np.float32), right.astype(np.float32)


def kernel(
    dims,
    box_ref,
    occ_ref,
    coup_ref,
    orb_ref,
    vin_ref,
    ion_ref,
    har_ref,
    proj_ref,
    left_ref,
    right_ref,
    app_ref,
    pot_ref,
    pprev,
    halo,
    hhalo,
    rhalo,
    dens_f,
    dens_b,
    dens_in,
    rho,
    chg1,
    chg2,
    chg3,
    chg_in1,
    chg_in2,
    chg_in3,
    scat,
    local_part,
    fields,
    gathered,
    turned,
    partial,
    weights,
    added,
    part_own,
    part_prev,
    got_own,
    got_prev,
    couple,
    hone,
    s_proj,
    r_proj,
    s_fwd,
    r_fwd,
    s_halo,
    r_halo,
    s_hh,
    r_hh,
    s_dens,
    r_dens,
    s_c1,
    r_c1,
    s_c2,
    r_c2,
    s_c3,
    r_c3,
    s_rh,
    r_rh,
    s_part,
    r_part,
):
    n_band, n_space, group = dims
    orbs, planes, rows, cols = orb_ref.shape
    atoms, nproj, width, square = proj_ref.shape
    cells = planes * rows
    n_far = n_space // group
    half = atoms // 2
    quarter = half // 2

    me_b = lax.axis_index("band")
    me_s = lax.axis_index("space")
    nxt = lax.rem(me_s + 1, n_space)
    prv = lax.rem(me_s + n_space - 1, n_space)
    core = lax.rem(me_b, 2)
    sib = me_b + 1 - 2 * core
    near = lax.rem(me_s, group)
    far = me_s // group

    def band_peer(d):
        return (lax.rem(me_b + d, n_band), me_s)

    def near_peer(d):
        return (me_b, far * group + lax.rem(near + d, group))

    def far_peer(d):
        return (me_b, lax.rem(far + d, n_far) * group + near)

    partners = [(me_b, nxt), (me_b, prv)]
    partners += [band_peer(d) for d in range(1, n_band)]
    partners += [near_peer(d) for d in range(1, group)]
    partners += [far_peer(d) for d in range(1, n_far)]
    barrier = pltpu.get_barrier_semaphore()
    for partner in partners:
        pl.semaphore_signal(barrier, inc=1, device_id=partner, device_id_type=MESH)
    pl.semaphore_wait(barrier, len(partners))

    sent = []

    def send(src, dst, send_sem, recv_sem, device):
        copy = pltpu.make_async_remote_copy(
            src_ref=src,
            dst_ref=dst,
            send_sem=send_sem,
            recv_sem=recv_sem,
            device_id=device,
            device_id_type=MESH,
        )
        copy.start()
        sent.append(copy)

    def arrived(dst, send_sem, recv_sem):
        pltpu.make_async_remote_copy(
            src_ref=dst,
            dst_ref=dst,
            send_sem=send_sem,
            recv_sem=recv_sem,
            device_id=(me_b, nxt),
            device_id_type=MESH,
        ).wait_recv()

    for h in range(2):
        some = pl.ds(core * half + h * quarter, quarter)
        send(proj_ref.at[some], pprev.at[some], s_proj.at[h], r_proj.at[h], (me_b, nxt))
    send(orb_ref.at[:, pl.ds(0, 2)], halo.at[1], s_halo.at[1], r_halo.at[1], (me_b, prv))
    send(har_ref.at[pl.ds(0, 2)], hhalo.at[1], s_hh.at[1], r_hh.at[1], (me_b, prv))
    send(har_ref.at[pl.ds(planes - 2, 2)], hhalo.at[0], s_hh.at[0], r_hh.at[0], (me_b, nxt))
    send(orb_ref.at[:, pl.ds(planes - 2, 2)], halo.at[0], s_halo.at[0], r_halo.at[0], (me_b, nxt))

    def density_plane(i, charge):
        total = jnp.zeros((rows, cols), F32)
        for o in range(orbs):
            field = orb_ref[o, i].astype(F32)
            at = (o * planes + i) * rows
            fields[pl.ds(pl.multiple_of(at, rows), rows), :] = field
            total = total + (occ_ref[o] * field) * field
        dens_f[i] = total
        dens_b[i] = total.astype(BF16)
        for r in range(0, rows, ROWGROUP):
            charge = charge + total[r : r + ROWGROUP]
        return charge

    chg1[...] = lax.fori_loop(0, planes, density_plane, jnp.zeros((ROWGROUP, cols), F32))
    for d in range(1, n_band):
        send(dens_b, dens_in.at[me_b], s_dens.at[d], r_dens.at[me_b], band_peer(d))
        send(chg1, chg_in1.at[me_b], s_c1.at[d], r_c1.at[me_b], band_peer(d))

    first_own = me_s * atoms
    first_prev = prv * atoms
    for part, first in ((0, first_own), (1, first_prev)):
        for a in range(atoms):
            want = lax.broadcasted_iota(jnp.int32, (SLOT, cols), 0) + box_ref[2, first + a]
            zcol = lax.broadcasted_iota(jnp.int32, (SLOT, cols), 1)
            at = (part * atoms + a) * SLOT
            scat[at : at + SLOT, :] = jnp.where(zcol == want, 1.0, 0.0).astype(BF16)

    def stencil(pair, carry):
        first, second = orb_ref[2 * pair], orb_ref[2 * pair + 1]
        both = jnp.concatenate([first.reshape(cells, cols), second.reshape(cells, cols)], axis=1)
        lap = jnp.dot(left_ref[...], both, preferred_element_type=F32)
        lap = lap + jnp.dot(both, right_ref[...], preferred_element_type=F32)
        vin = vin_ref[...].reshape(cells, cols)
        for n in range(2):
            field = both[:, n * cols : (n + 1) * cols].astype(F32)
            local_part[2 * pair + n] = lap[:, n * cols : (n + 1) * cols] * (-0.5 / 12.0) + vin * field
        return carry

    lax.fori_loop(0, orbs // 2, stencil, 0)

    def boxes(y, carry):
        line = fields[pl.ds(y, orbs * planes, stride=rows), :].astype(BF16)
        cut = lax.dot_general(
            scat[...], line, (((1,), (1,)), ((), ())), preferred_element_type=F32
        ).astype(BF16)
        at = pl.ds(pl.multiple_of(y * SLOT, SLOT), SLOT)
        for n in range(2 * atoms):
            gathered[n, at, :] = cut[n * SLOT : (n + 1) * SLOT, :]
        return carry

    lax.fori_loop(0, rows, boxes, 0)

    for d in range(1, n_band):
        peer = lax.rem(me_b + d, n_band)
        arrived(chg_in1.at[peer], s_c1.at[d], r_c1.at[peer])
    charge = chg1[...]
    for d in range(1, n_band):
        charge = charge + chg_in1[lax.rem(me_b + d, n_band)]
    chg2[...] = charge
    for d in range(1, group):
        send(chg2, chg_in2.at[near], s_c2.at[d], r_c2.at[near], near_peer(d))
    for d in range(1, n_band):
        peer = lax.rem(me_b + d, n_band)
        arrived(dens_in.at[peer], s_dens.at[d], r_dens.at[peer])
    total_density = dens_f[...]
    for d in range(1, n_band):
        total_density = total_density + dens_in[lax.rem(me_b + d, n_band)].astype(F32)
    rho[...] = total_density
    send(rho.at[0], rhalo.at[1], s_rh.at[1], r_rh.at[1], (me_b, prv))
    send(rho.at[planes - 1], rhalo.at[0], s_rh.at[0], r_rh.at[0], (me_b, nxt))

    wide = orbs * planes
    belongs = jnp.where(
        lax.broadcasted_iota(jnp.int32, (orbs, wide), 1) // planes
        == lax.broadcasted_iota(jnp.int32, (orbs, wide), 0),
        1.0,
        0.0,
    ).astype(BF16)
    step = (
        lax.broadcasted_iota(jnp.int32, (width, wide), 1) % planes
        - lax.broadcasted_iota(jnp.int32, (width, wide), 0)
    )

    def on_plane(part, first, a):
        return step == lax.rem(box_ref[0, first + a], planes) - part * planes

    def gather(part, source, first):
        for a in range(atoms):
            beta = source[a].reshape(nproj * width, square)
            turned[part * atoms + a] = beta.T
            pairs = jnp.dot(beta, gathered[part * atoms + a], preferred_element_type=F32)
            pairs = jnp.where(
                on_plane(part, first, a)[None], pairs.reshape(nproj, width, wide), 0.0
            )
            folded = pairs[:, :ROWGROUP] + pairs[:, ROWGROUP:]
            folded = folded.reshape(nproj * ROWGROUP, wide)
            at = a * nproj * ROWGROUP
            for t in range(wide // cols):
                partial[t, at : at + nproj * ROWGROUP] = folded[:, t * cols : (t + 1) * cols]
        count = atoms * nproj
        tiles = []
        for t in range(wide // cols):
            total = partial[t, pl.ds(0, count, stride=ROWGROUP), :]
            for r in range(1, ROWGROUP):
                total = total + partial[t, pl.ds(r, count, stride=ROWGROUP), :]
            tiles.append(total)
        total = jnp.concatenate(tiles, axis=1)
        total = jnp.concatenate([total, jnp.zeros((cols - count, wide), F32)], axis=0)
        high = total.astype(BF16)
        low = (total - high.astype(F32)).astype(BF16)
        lanes = (((1,), (1,)), ((), ()))
        return lax.dot_general(
            belongs, high, lanes, preferred_element_type=F32
        ) + lax.dot_general(belongs, low, lanes, preferred_element_type=F32)

    part_own[...] = gather(0, proj_ref, first_own)
    send(part_own, got_prev, s_part.at[0], r_part.at[0], (me_b, nxt))

    for d in range(1, group):
        peer = lax.rem(near + d, group)
        arrived(chg_in2.at[peer], s_c2.at[d], r_c2.at[peer])
    charge = chg2[...]
    for d in range(1, group):
        charge = charge + chg_in2[lax.rem(near + d, group)]
    chg3[...] = charge
    for d in range(1, n_far):
        send(chg3, chg_in3.at[far], s_c3.at[d], r_c3.at[far], far_peer(d))

    for h in range(2):
        some = pl.ds(core * half + h * quarter, quarter)
        arrived(pprev.at[some], s_proj.at[h], r_proj.at[h])
        send(pprev.at[some], pprev.at[some], s_fwd.at[h], r_fwd.at[h], (sib, me_s))
    for h in range(2):
        some = pl.ds((1 - core) * half + h * quarter, quarter)
        arrived(pprev.at[some], s_fwd.at[h], r_fwd.at[h])
    part_prev[...] = gather(1, pprev, first_prev)
    send(part_prev, got_own, s_part.at[1], r_part.at[1], (me_b, prv))

    for side in range(2):
        arrived(hhalo.at[side], s_hh.at[side], r_hh.at[side])
        arrived(rhalo.at[side], s_rh.at[side], r_rh.at[side])

    def around(cell):
        return (
            pltpu.roll(cell, 1, 0)
            + pltpu.roll(cell, rows - 1, 0)
            + pltpu.roll(cell, 1, 1)
            + pltpu.roll(cell, cols - 1, 1)
        )

    def start_plane(p):
        if p < 0:
            return hhalo[0, p + 2]
        if p >= planes:
            return hhalo[1, p - planes]
        return har_ref[p]

    def rho_plane(p):
        if p < 0:
            return rhalo[0]
        if p >= planes:
            return rhalo[1]
        return rho[p]

    inverse = 1.0 / (6.0 + SCREENING)
    for p in range(-1, planes + 1):
        total = start_plane(p - 1) + start_plane(p + 1) + around(start_plane(p))
        hone[p + 1] = (total + FOUR_PI * rho_plane(p)) * inverse
    for d in range(1, n_far):
        peer = lax.rem(far + d, n_far)
        arrived(chg_in3.at[peer], s_c3.at[d], r_c3.at[peer])
    charge = chg3[...]
    for d in range(1, n_far):
        charge = charge + chg_in3[lax.rem(far + d, n_far)]
    mean = jnp.sum(charge, axis=(0, 1), keepdims=True) * (1.0 / (cells * cols * n_space))
    lift = FOUR_PI * inverse * (1.0 + 6.0 * inverse) * mean
    for p in range(planes):
        total = hone[p] + hone[p + 2] + around(hone[p + 1])
        second = (total + FOUR_PI * rho[p]) * inverse
        root = jnp.exp(jnp.log(rho[p] * (3.0 / math.pi)) * (1.0 / 3.0))
        pot_ref[p] = ion_ref[p] + (second - lift) - root

    for side in range(2):
        arrived(halo.at[side], s_halo.at[side], r_halo.at[side])

    def edges(o, carry):
        near_low, far_low = halo[0, o, 1].astype(F32), halo[0, o, 0].astype(F32)
        near_up, far_up = halo[1, o, 0].astype(F32), halo[1, o, 1].astype(F32)
        scale = -0.5 / 12.0
        last = cells - rows
        local_part[o, 0:rows] += scale * (16.0 * near_low - far_low)
        local_part[o, rows : 2 * rows] += (-scale) * near_low
        local_part[o, last : last + rows] += scale * (16.0 * near_up - far_up)
        local_part[o, last - rows : last] += (-scale) * near_up
        return carry

    lax.fori_loop(0, orbs, edges, 0)

    row_id = lax.broadcasted_iota(jnp.int32, (cols, nproj), 0) % nproj
    pick = jnp.where(
        row_id == lax.broadcasted_iota(jnp.int32, (cols, nproj), 1), 1.0, 0.0
    ).astype(F32)
    tall = jnp.dot(
        pick, coup_ref[...], precision=lax.Precision.HIGHEST, preferred_element_type=F32
    )
    full = lax.dot_general(
        tall,
        pick,
        (((1,), (1,)), ((), ())),
        precision=lax.Precision.HIGHEST,
        preferred_element_type=F32,
    )
    same = (
        lax.broadcasted_iota(jnp.int32, (cols, cols), 0) // nproj
        == lax.broadcasted_iota(jnp.int32, (cols, cols), 1) // nproj
    )
    couple[...] = jnp.where(same, full, 0.0)

    arrived(got_prev, s_part.at[0], r_part.at[0])
    arrived(got_own, s_part.at[1], r_part.at[1])
    for part, mine, other, first in (
        (0, part_own, got_own, first_own),
        (1, part_prev, got_prev, first_prev),
    ):
        weighted = lax.dot_general(
            couple[...],
            mine[...] + other[...],
            (((1,), (1,)), ((), ())),
            precision=lax.Precision.HIGHEST,
            preferred_element_type=F32,
        ).astype(BF16)
        weights[...] = jnp.dot(weighted, belongs, preferred_element_type=F32)
        for a in range(atoms):
            rows_a = weights[a * nproj : (a + 1) * nproj, :].reshape(nproj, 1, wide)
            placed = jnp.where(on_plane(part, first, a)[None], rows_a, 0.0)
            placed = placed.reshape(nproj * width, wide).astype(BF16)
            term = jnp.dot(
                turned[part * atoms + a], placed, preferred_element_type=F32
            ).astype(BF16)
            at = (part * atoms + a) * SLOT
            for y in range(rows):
                added[y, at : at + SLOT, :] = term[y * SLOT : (y + 1) * SLOT, :]

    def scatter(y, carry):
        fields[pl.ds(y, wide, stride=rows), :] = lax.dot_general(
            added[y], scat[...], (((0,), (0,)), ((), ())), preferred_element_type=F32
        )
        return carry

    lax.fori_loop(0, rows, scatter, 0)

    def finish(o, carry):
        at = pl.ds(pl.multiple_of(o * cells, cells), cells)
        total = local_part[o] + fields[at, :]
        app_ref[o] = total.astype(BF16).reshape(planes, rows, cols)
        return carry

    lax.fori_loop(0, orbs, finish, 0)

    for copy in sent:
        copy.wait_send()


def local(
    n_band,
    n_space,
    orbitals,
    occupations,
    potential_in,
    ionic_potential,
    hartree_prev,
    projectors,
    box_start,
    coupling,
):
    orbs, planes, rows, cols = orbitals.shape
    atoms, nproj, width, square = projectors.shape
    cells = planes * rows
    group = 8 if n_space % 8 == 0 else 2
    n_far = n_space // group
    left, right = stencil_matrices(planes, rows, cols)
    vmem = pl.BlockSpec(memory_space=pltpu.VMEM)
    smem = pl.BlockSpec(memory_space=pltpu.SMEM)
    dma = pltpu.SemaphoreType.DMA
    scratch = [
        pltpu.VMEM(projectors.shape, BF16),
        pltpu.VMEM((2, orbs, 2, rows, cols), BF16),
        pltpu.VMEM((2, 2, rows, cols), F32),
        pltpu.VMEM((2, rows, cols), F32),
        pltpu.VMEM((planes, rows, cols), F32),
        pltpu.VMEM((planes, rows, cols), BF16),
        pltpu.VMEM((n_band, planes, rows, cols), BF16),
        pltpu.VMEM((planes, rows, cols), F32),
        pltpu.VMEM((ROWGROUP, cols), F32),
        pltpu.VMEM((ROWGROUP, cols), F32),
        pltpu.VMEM((ROWGROUP, cols), F32),
        pltpu.VMEM((n_band, ROWGROUP, cols), F32),
        pltpu.VMEM((group, ROWGROUP, cols), F32),
        pltpu.VMEM((n_far, ROWGROUP, cols), F32),
        pltpu.VMEM((2 * atoms * SLOT, cols), BF16),
        pltpu.VMEM((orbs, cells, cols), F32),
        pltpu.VMEM((orbs * cells, cols), F32),
        pltpu.VMEM((2 * atoms, square, orbs * planes), BF16),
        pltpu.VMEM((2 * atoms, square, nproj * width), BF16),
        pltpu.VMEM((orbs * planes // cols, atoms * nproj * ROWGROUP, cols), F32),
        pltpu.VMEM((cols, orbs * planes), F32),
        pltpu.VMEM((rows, 2 * atoms * SLOT, orbs * planes), BF16),
        pltpu.VMEM((orbs, cols), F32),
        pltpu.VMEM((orbs, cols), F32),
        pltpu.VMEM((orbs, cols), F32),
        pltpu.VMEM((orbs, cols), F32),
        pltpu.VMEM((cols, cols), F32),
        pltpu.VMEM((planes + 2, rows, cols), F32),
        dma((2,)),
        dma((2,)),
        dma((2,)),
        dma((2,)),
        dma((2,)),
        dma((2,)),
        dma((2,)),
        dma((2,)),
        dma((n_band,)),
        dma((n_band,)),
        dma((n_band,)),
        dma((n_band,)),
        dma((group,)),
        dma((group,)),
        dma((n_far,)),
        dma((n_far,)),
        dma((2,)),
        dma((2,)),
        dma((2,)),
        dma((2,)),
    ]
    return pl.pallas_call(
        functools.partial(kernel, (n_band, n_space, group)),
        out_shape=(
            jax.ShapeDtypeStruct(orbitals.shape, BF16),
            jax.ShapeDtypeStruct(potential_in.shape, F32),
        ),
        in_specs=[smem, smem] + [vmem] * 8,
        out_specs=(vmem, vmem),
        scratch_shapes=scratch,
        compiler_params=pltpu.CompilerParams(
            collective_id=0, has_side_effects=True, vmem_limit_bytes=56 * 1024 * 1024
        ),
    )(
        box_start,
        occupations,
        coupling,
        orbitals,
        potential_in,
        ionic_potential,
        hartree_prev,
        projectors,
        jnp.asarray(left, BF16),
        jnp.asarray(right, BF16),
    )


def solution(mesh):
    return jax.shard_map(
        functools.partial(local, mesh.shape["band"], mesh.shape["space"]),
        mesh=mesh,
        in_specs=(
            P("band", "space", None, None),
            P("band"),
            P("space", None, None),
            P("space", None, None),
            P("space", None, None),
            P("space", None, None, None),
            P(),
            P(),
        ),
        out_specs=(P("band", "space", None, None), P("space", None, None)),
        check_vma=False,
    )
```

```python
import functools
import math

import jax
import jax.numpy as jnp
import numpy as np
from jax import lax
from jax.experimental import pallas as pl
from jax.experimental.pallas import tpu as pltpu
from jax.sharding import PartitionSpec as P

SCREENING = 0.25
SWEEPS = 2
FOUR_PI = 4.0 * math.pi
ROWGROUP = 8
MESH = pl.DeviceIdType.MESH
F32 = jnp.float32
BF16 = jnp.bfloat16
SLOT = 16


def stencil_matrices(planes, rows, cols):
    def line(count, periodic):
        matrix = np.zeros((count, count), np.float32)
        for distance, weight in ((1, 16.0), (2, -1.0)):
            for sign in (-1, 1):
                for index in range(count):
                    other = index + sign * distance
                    if periodic:
                        other %= count
                    if 0 <= other < count:
                        matrix[index, other] += weight
        return matrix

    left = np.kron(line(planes, False), np.eye(rows)) + np.kron(np.eye(planes), line(rows, True))
    right = np.kron(np.eye(2), line(cols, True) - 90.0 * np.eye(cols))
    return left.astype(np.float32), right.astype(np.float32)


def tables(box_ref, first_own, first_prev, scat, atoms, cols):
    for part, first in ((0, first_own), (1, first_prev)):
        for a in range(atoms):
            want = lax.broadcasted_iota(jnp.int32, (SLOT, cols), 0) + box_ref[2, first + a]
            zcol = lax.broadcasted_iota(jnp.int32, (SLOT, cols), 1)
            at = (part * atoms + a) * SLOT
            scat[at : at + SLOT, :] = jnp.where(zcol == want, 1.0, 0.0).astype(BF16)


def ownership(orbs, wide, planes):
    lane = lax.broadcasted_iota(jnp.int32, (orbs, wide), 1) // planes
    own = lane == lax.broadcasted_iota(jnp.int32, (orbs, wide), 0)
    return jnp.where(own, 1.0, 0.0).astype(BF16)


def plane_steps(width, wide, planes):
    lane = lax.broadcasted_iota(jnp.int32, (width, wide), 1) % planes
    return lane - lax.broadcasted_iota(jnp.int32, (width, wide), 0)


def exchange(
    dims,
    box_ref,
    occ_ref,
    coup_ref,
    orb_hbm,
    vin_hbm,
    har_hbm,
    proj_hbm,
    left_hbm,
    right_hbm,
    local_out,
    turned_out,
    halo,
    weighted_out,
    pre_ref,
    orb_ref,
    vin_ref,
    har_ref,
    proj_ref,
    left_ref,
    right_ref,
    pprev,
    hhalo,
    rhalo,
    dens_f,
    dens_b,
    dens_in,
    rho,
    chg1,
    chg2,
    chg3,
    chg_in1,
    chg_in2,
    chg_in3,
    scat,
    local_part,
    fields,
    gathered,
    turned,
    partial,
    part_own,
    part_prev,
    got_own,
    got_prev,
    couple,
    hone,
    s_load,
    s_store,
    s_proj,
    r_proj,
    s_fwd,
    r_fwd,
    s_halo,
    r_halo,
    s_hh,
    r_hh,
    s_dens,
    r_dens,
    s_c1,
    r_c1,
    s_c2,
    r_c2,
    s_c3,
    r_c3,
    s_rh,
    r_rh,
    s_part,
    r_part,
):
    n_band, n_space, group = dims
    orbs, planes, rows, cols = orb_ref.shape
    atoms, nproj, width, square = proj_ref.shape
    cells = planes * rows
    wide = orbs * planes
    n_far = n_space // group
    half = atoms // 2

    me_b = lax.axis_index("band")
    me_s = lax.axis_index("space")
    nxt = lax.rem(me_s + 1, n_space)
    prv = lax.rem(me_s + n_space - 1, n_space)
    core = lax.rem(me_b, 2)
    sib = me_b + 1 - 2 * core
    near = lax.rem(me_s, group)
    far = me_s // group

    def band_peer(d):
        return (lax.rem(me_b + d, n_band), me_s)

    def near_peer(d):
        return (me_b, far * group + lax.rem(near + d, group))

    def far_peer(d):
        return (me_b, lax.rem(far + d, n_far) * group + near)

    partners = [(me_b, nxt), (me_b, prv)]
    partners += [band_peer(d) for d in range(1, n_band)]
    partners += [near_peer(d) for d in range(1, group)]
    partners += [far_peer(d) for d in range(1, n_far)]
    barrier = pltpu.get_barrier_semaphore()
    for partner in partners:
        pl.semaphore_signal(barrier, inc=1, device_id=partner, device_id_type=MESH)

    loads = []
    for n, (src, dst) in enumerate(
        (
            (orb_hbm, orb_ref),
            (proj_hbm, proj_ref),
            (left_hbm, left_ref),
            (right_hbm, right_ref),
            (vin_hbm, vin_ref),
            (har_hbm, har_ref),
        )
    ):
        loads.append(pltpu.make_async_copy(src, dst, s_load.at[n]))
        loads[n].start()

    pl.semaphore_wait(barrier, len(partners))

    sent = []

    def send(src, dst, send_sem, recv_sem, device):
        copy = pltpu.make_async_remote_copy(
            src_ref=src,
            dst_ref=dst,
            send_sem=send_sem,
            recv_sem=recv_sem,
            device_id=device,
            device_id_type=MESH,
        )
        copy.start()
        sent.append(copy)

    def arrived(dst, send_sem, recv_sem):
        pltpu.make_async_remote_copy(
            src_ref=dst,
            dst_ref=dst,
            send_sem=send_sem,
            recv_sem=recv_sem,
            device_id=(me_b, nxt),
            device_id_type=MESH,
        ).wait_recv()

    for h in range(half):
        a = core * half + h
        send(proj_hbm.at[a], pprev.at[a], s_proj.at[h], r_proj.at[h], (me_b, nxt))
    send(har_hbm.at[pl.ds(0, 2)], hhalo.at[1], s_hh.at[1], r_hh.at[1], (me_b, prv))
    send(har_hbm.at[pl.ds(planes - 2, 2)], hhalo.at[0], s_hh.at[0], r_hh.at[0], (me_b, nxt))
    first_own = me_s * atoms
    first_prev = prv * atoms
    tables(box_ref, first_own, first_prev, scat, atoms, cols)

    loads[0].wait()

    def density_plane(i, charge):
        total = jnp.zeros((rows, cols), F32)
        for o in range(orbs):
            field = orb_ref[o, i].astype(F32)
            at = (o * planes + i) * rows
            fields[pl.ds(pl.multiple_of(at, rows), rows), :] = field
            total = total + (occ_ref[o] * field) * field
        dens_f[i] = total
        dens_b[i] = total.astype(BF16)
        for r in range(0, rows, ROWGROUP):
            charge = charge + total[r : r + ROWGROUP]
        return charge

    chg1[...] = lax.fori_loop(0, planes, density_plane, jnp.zeros((ROWGROUP, cols), F32))
    for d in range(1, n_band):
        send(chg1, chg_in1.at[me_b], s_c1.at[d], r_c1.at[me_b], band_peer(d))
    for d in range(1, n_band):
        send(dens_b, dens_in.at[me_b], s_dens.at[d], r_dens.at[me_b], band_peer(d))
    send(orb_ref.at[:, pl.ds(0, 2)], halo.at[1], s_halo.at[1], r_halo.at[1], (me_b, prv))
    send(orb_ref.at[:, pl.ds(planes - 2, 2)], halo.at[0], s_halo.at[0], r_halo.at[0], (me_b, nxt))

    for y in range(rows):
        line = fields[pl.ds(y, wide, stride=rows), :].astype(BF16)
        cut = lax.dot_general(
            scat[...], line, (((1,), (1,)), ((), ())), preferred_element_type=F32
        ).astype(BF16)
        for n in range(2 * atoms):
            gathered[n, y * SLOT : (y + 1) * SLOT, :] = cut[n * SLOT : (n + 1) * SLOT, :]

    for d in range(1, n_band):
        peer = lax.rem(me_b + d, n_band)
        arrived(chg_in1.at[peer], s_c1.at[d], r_c1.at[peer])
    charge = chg1[...]
    for d in range(1, n_band):
        charge = charge + chg_in1[lax.rem(me_b + d, n_band)]
    chg2[...] = charge
    for d in range(1, group):
        send(chg2, chg_in2.at[near], s_c2.at[d], r_c2.at[near], near_peer(d))

    belongs = ownership(orbs, wide, planes)
    step = plane_steps(width, wide, planes)

    def gather(part, source, first, a):
        beta = source[a].reshape(nproj * width, square)
        turned[part * atoms + a] = beta.T
        pairs = jnp.dot(beta, gathered[part * atoms + a], preferred_element_type=F32)
        keep = step == lax.rem(box_ref[0, first + a], planes) - part * planes
        pairs = jnp.where(keep[None], pairs.reshape(nproj, width, wide), 0.0)
        folded = pairs[:, :ROWGROUP] + pairs[:, ROWGROUP:]
        folded = folded.reshape(nproj * ROWGROUP, wide)
        at = pl.ds(pl.multiple_of(a * nproj * ROWGROUP, ROWGROUP), nproj * ROWGROUP)
        for t in range(wide // cols):
            partial[t, at, :] = folded[:, t * cols : (t + 1) * cols]

    def gathered_sum():
        count = atoms * nproj
        tiles = []
        for t in range(wide // cols):
            total = partial[t, pl.ds(0, count, stride=ROWGROUP), :]
            for r in range(1, ROWGROUP):
                total = total + partial[t, pl.ds(r, count, stride=ROWGROUP), :]
            tiles.append(total)
        total = jnp.concatenate(tiles, axis=1)
        total = jnp.concatenate([total, jnp.zeros((cols - count, wide), F32)], axis=0)
        high = total.astype(BF16)
        low = (total - high.astype(F32)).astype(BF16)
        lanes = (((1,), (1,)), ((), ()))
        return lax.dot_general(
            belongs, high, lanes, preferred_element_type=F32
        ) + lax.dot_general(belongs, low, lanes, preferred_element_type=F32)

    def hand_on(h):
        a = core * half + h
        arrived(pprev.at[a], s_proj.at[h], r_proj.at[h])
        send(pprev.at[a], pprev.at[a], s_fwd.at[h], r_fwd.at[h], (sib, me_s))

    loads[1].wait()
    for a in range(atoms):
        gather(0, proj_ref, first_own, a)
    part_own[...] = gathered_sum()
    send(part_own, got_prev, s_part.at[0], r_part.at[0], (me_b, nxt))

    hand_on(0)

    for n in range(2, 5):
        loads[n].wait()
    for pair in range(orbs // 2):
        first, second = orb_ref[2 * pair], orb_ref[2 * pair + 1]
        both = jnp.concatenate([first.reshape(cells, cols), second.reshape(cells, cols)], axis=1)
        lap = jnp.dot(left_ref[...], both, preferred_element_type=F32)
        lap = lap + jnp.dot(both, right_ref[...], preferred_element_type=F32)
        vin = vin_ref[...].reshape(cells, cols)
        for n in range(2):
            field = both[:, n * cols : (n + 1) * cols].astype(F32)
            local_part[2 * pair + n] = lap[:, n * cols : (n + 1) * cols] * (-0.5 / 12.0) + vin * field
    stores = [
        pltpu.make_async_copy(local_part, local_out, s_store.at[0]),
        pltpu.make_async_copy(
            turned.at[pl.ds(0, atoms)], turned_out.at[pl.ds(0, atoms)], s_store.at[1]
        ),
        pltpu.make_async_copy(
            turned.at[pl.ds(atoms, atoms)], turned_out.at[pl.ds(atoms, atoms)], s_store.at[2]
        ),
    ]
    stores[0].start()
    stores[1].start()

    hand_on(1)

    for d in range(1, n_band):
        peer = lax.rem(me_b + d, n_band)
        arrived(dens_in.at[peer], s_dens.at[d], r_dens.at[peer])
    total_density = dens_f[...]
    for d in range(1, n_band):
        total_density = total_density + dens_in[lax.rem(me_b + d, n_band)].astype(F32)
    rho[...] = total_density
    send(rho.at[0], rhalo.at[1], s_rh.at[1], r_rh.at[1], (me_b, prv))
    send(rho.at[planes - 1], rhalo.at[0], s_rh.at[0], r_rh.at[0], (me_b, nxt))
    for d in range(1, group):
        peer = lax.rem(near + d, group)
        arrived(chg_in2.at[peer], s_c2.at[d], r_c2.at[peer])
    charge = chg2[...]
    for d in range(1, group):
        charge = charge + chg_in2[lax.rem(near + d, group)]
    chg3[...] = charge
    for d in range(1, n_far):
        send(chg3, chg_in3.at[far], s_c3.at[d], r_c3.at[far], far_peer(d))

    for h in range(2, half):
        hand_on(h)
        gather(1, pprev, first_prev, core * half + h - 2)
    for h in range(half):
        a = (1 - core) * half + h
        arrived(pprev.at[a], s_fwd.at[h], r_fwd.at[h])
        gather(1, pprev, first_prev, a)
        if h < 2:
            gather(1, pprev, first_prev, core * half + half - 2 + h)
    part_prev[...] = gathered_sum()
    send(part_prev, got_own, s_part.at[1], r_part.at[1], (me_b, prv))
    stores[2].start()

    loads[5].wait()
    for side in range(2):
        arrived(hhalo.at[side], s_hh.at[side], r_hh.at[side])
        arrived(rhalo.at[side], s_rh.at[side], r_rh.at[side])

    def around(cell):
        return (
            pltpu.roll(cell, 1, 0)
            + pltpu.roll(cell, rows - 1, 0)
            + pltpu.roll(cell, 1, 1)
            + pltpu.roll(cell, cols - 1, 1)
        )

    def start_plane(p):
        if p < 0:
            return hhalo[0, p + 2]
        if p >= planes:
            return hhalo[1, p - planes]
        return har_ref[p]

    def rho_plane(p):
        if p < 0:
            return rhalo[0]
        if p >= planes:
            return rhalo[1]
        return rho[p]

    inverse = 1.0 / (6.0 + SCREENING)
    for p in range(-1, planes + 1):
        total = start_plane(p - 1) + start_plane(p + 1) + around(start_plane(p))
        hone[p + 1] = (total + FOUR_PI * rho_plane(p)) * inverse
    for d in range(1, n_far):
        peer = lax.rem(far + d, n_far)
        arrived(chg_in3.at[peer], s_c3.at[d], r_c3.at[peer])
    charge = chg3[...]
    for d in range(1, n_far):
        charge = charge + chg_in3[lax.rem(far + d, n_far)]
    mean = jnp.sum(charge, axis=(0, 1), keepdims=True) * (1.0 / (cells * cols * n_space))
    lift = FOUR_PI * inverse * (1.0 + 6.0 * inverse) * mean
    for p in range(planes):
        total = hone[p] + hone[p + 2] + around(hone[p + 1])
        second = (total + FOUR_PI * rho[p]) * inverse
        root = jnp.exp(jnp.log(rho[p] * (3.0 / math.pi)) * (1.0 / 3.0))
        pre_ref[p] = (second - lift) - root

    row_id = lax.broadcasted_iota(jnp.int32, (cols, nproj), 0) % nproj
    pick = jnp.where(
        row_id == lax.broadcasted_iota(jnp.int32, (cols, nproj), 1), 1.0, 0.0
    ).astype(F32)
    tall = jnp.dot(
        pick, coup_ref[...], precision=lax.Precision.HIGHEST, preferred_element_type=F32
    )
    full = lax.dot_general(
        tall,
        pick,
        (((1,), (1,)), ((), ())),
        precision=lax.Precision.HIGHEST,
        preferred_element_type=F32,
    )
    same = (
        lax.broadcasted_iota(jnp.int32, (cols, cols), 0) // nproj
        == lax.broadcasted_iota(jnp.int32, (cols, cols), 1) // nproj
    )
    couple[...] = jnp.where(same, full, 0.0)

    arrived(got_prev, s_part.at[0], r_part.at[0])
    arrived(got_own, s_part.at[1], r_part.at[1])
    for part, mine, other in ((0, part_own, got_own), (1, part_prev, got_prev)):
        weighted_out[part] = lax.dot_general(
            couple[...],
            mine[...] + other[...],
            (((1,), (1,)), ((), ())),
            precision=lax.Precision.HIGHEST,
            preferred_element_type=F32,
        )

    for side in range(2):
        arrived(halo.at[side], s_halo.at[side], r_halo.at[side])
    for copy in sent:
        copy.wait_send()
    for copy in stores:
        copy.wait()


def apply_terms(
    n_space,
    box_ref,
    weighted_ref,
    pre_ref,
    ion_ref,
    local_hbm,
    turned_hbm,
    halo_hbm,
    app_hbm,
    pot_ref,
    local_part,
    turned,
    halo,
    app_ref,
    scat,
    weights,
    added,
    nonlocal_part,
    s_turned,
    s_local,
    s_halo,
    s_app,
):
    orbs, planes, rows, cols = app_ref.shape
    cells = planes * rows
    wide = orbs * planes
    atoms2, square, depth = turned.shape
    atoms = atoms2 // 2
    width = planes
    nproj = depth // width
    me_s = lax.axis_index("space")
    prv = lax.rem(me_s + n_space - 1, n_space)
    firsts = (me_s * atoms, prv * atoms)
    pieces = s_turned.shape[0]
    lot = atoms2 // pieces
    batches = s_local.shape[0]
    some = orbs // batches

    loads_t = []
    for n in range(pieces):
        at = pl.ds(n * lot, lot)
        loads_t.append(pltpu.make_async_copy(turned_hbm.at[at], turned.at[at], s_turned.at[n]))
    loads_l = []
    for n in range(batches):
        at = pl.ds(n * some, some)
        loads_l.append(pltpu.make_async_copy(local_hbm.at[at], local_part.at[at], s_local.at[n]))
    load_h = pltpu.make_async_copy(halo_hbm, halo, s_halo)
    for copy in loads_t:
        copy.start()
    load_h.start()
    for copy in loads_l:
        copy.start()

    tables(box_ref, firsts[0], firsts[1], scat, atoms, cols)
    belongs = ownership(orbs, wide, planes)
    step = plane_steps(width, wide, planes)
    for part in range(2):
        weights[part] = jnp.dot(
            weighted_ref[part].astype(BF16), belongs, preferred_element_type=F32
        )
    pot_ref[...] = ion_ref[...] + pre_ref[...]
    for n in range(atoms2):
        if n % lot == 0:
            loads_t[n // lot].wait()
        part, a = n // atoms, n % atoms
        keep = step == lax.rem(box_ref[0, firsts[part] + a], planes) - part * planes
        rows_a = weights[part, a * nproj : (a + 1) * nproj, :].reshape(nproj, 1, wide)
        placed = jnp.where(keep[None], rows_a, 0.0)
        placed = placed.reshape(nproj * width, wide).astype(BF16)
        term = jnp.dot(turned[n], placed, preferred_element_type=F32).astype(BF16)
        for y in range(rows):
            added[y, n * SLOT : (n + 1) * SLOT, :] = term[y * SLOT : (y + 1) * SLOT, :]

    for y in range(rows):
        nonlocal_part[pl.ds(y, wide, stride=rows), :] = lax.dot_general(
            added[y], scat[...], (((0,), (0,)), ((), ())), preferred_element_type=F32
        )

    load_h.wait()
    outs = []
    scale = -0.5 / 12.0
    for n in range(batches):
        loads_l[n].wait()

        def finish(o, carry):
            near_low, far_low = halo[0, o, 1].astype(F32), halo[0, o, 0].astype(F32)
            near_up, far_up = halo[1, o, 0].astype(F32), halo[1, o, 1].astype(F32)
            edge = {
                0: scale * (16.0 * near_low - far_low),
                1: (-scale) * near_low,
                planes - 2: (-scale) * near_up,
                planes - 1: scale * (16.0 * near_up - far_up),
            }
            for i in range(planes):
                at = pl.ds(pl.multiple_of(o * cells + i * rows, rows), rows)
                total = local_part[o, i * rows : (i + 1) * rows, :] + nonlocal_part[at, :]
                if i in edge:
                    total = total + edge[i]
                app_ref[o, i] = total.astype(BF16)
            return carry

        lax.fori_loop(n * some, (n + 1) * some, finish, 0)
        at = pl.ds(n * some, some)
        outs.append(pltpu.make_async_copy(app_ref.at[at], app_hbm.at[at], s_app.at[n]))
        outs[n].start()
    for copy in outs:
        copy.wait()


def local(
    n_band,
    n_space,
    orbitals,
    occupations,
    potential_in,
    ionic_potential,
    hartree_prev,
    projectors,
    box_start,
    coupling,
):
    orbs, planes, rows, cols = orbitals.shape
    atoms, nproj, width, square = projectors.shape
    cells = planes * rows
    wide = orbs * planes
    group = 8 if n_space % 8 == 0 else 2
    n_far = n_space // group
    half = atoms // 2
    left, right = stencil_matrices(planes, rows, cols)
    left, right = jnp.asarray(left, BF16), jnp.asarray(right, BF16)
    vmem = pl.BlockSpec(memory_space=pltpu.VMEM)
    smem = pl.BlockSpec(memory_space=pltpu.SMEM)
    anywhere = pl.BlockSpec(memory_space=pl.ANY)
    dma = pltpu.SemaphoreType.DMA
    grid_f32 = jax.ShapeDtypeStruct(potential_in.shape, F32)
    halo_shape = (2, orbs, 2, rows, cols)
    turned_shape = (2 * atoms, square, nproj * width)
    scratch = [
        pltpu.VMEM(orbitals.shape, BF16),
        pltpu.VMEM(potential_in.shape, F32),
        pltpu.VMEM(hartree_prev.shape, F32),
        pltpu.VMEM(projectors.shape, BF16),
        pltpu.VMEM(left.shape, BF16),
        pltpu.VMEM(right.shape, BF16),
        pltpu.VMEM(projectors.shape, BF16),
        pltpu.VMEM((2, 2, rows, cols), F32),
        pltpu.VMEM((2, rows, cols), F32),
        pltpu.VMEM((planes, rows, cols), F32),
        pltpu.VMEM((planes, rows, cols), BF16),
        pltpu.VMEM((n_band, planes, rows, cols), BF16),
        pltpu.VMEM((planes, rows, cols), F32),
        pltpu.VMEM((ROWGROUP, cols), F32),
        pltpu.VMEM((ROWGROUP, cols), F32),
        pltpu.VMEM((ROWGROUP, cols), F32),
        pltpu.VMEM((n_band, ROWGROUP, cols), F32),
        pltpu.VMEM((group, ROWGROUP, cols), F32),
        pltpu.VMEM((n_far, ROWGROUP, cols), F32),
        pltpu.VMEM((2 * atoms * SLOT, cols), BF16),
        pltpu.VMEM((orbs, cells, cols), F32),
        pltpu.VMEM((orbs * cells, cols), F32),
        pltpu.VMEM((2 * atoms, square, wide), BF16),
        pltpu.VMEM(turned_shape, BF16),
        pltpu.VMEM((wide // cols, atoms * nproj * ROWGROUP, cols), F32),
        pltpu.VMEM((orbs, cols), F32),
        pltpu.VMEM((orbs, cols), F32),
        pltpu.VMEM((orbs, cols), F32),
        pltpu.VMEM((orbs, cols), F32),
        pltpu.VMEM((cols, cols), F32),
        pltpu.VMEM((planes + 2, rows, cols), F32),
        dma((6,)),
        dma((3,)),
        dma((half,)),
        dma((half,)),
        dma((half,)),
        dma((half,)),
        dma((2,)),
        dma((2,)),
        dma((2,)),
        dma((2,)),
        dma((n_band,)),
        dma((n_band,)),
        dma((n_band,)),
        dma((n_band,)),
        dma((group,)),
        dma((group,)),
        dma((n_far,)),
        dma((n_far,)),
        dma((2,)),
        dma((2,)),
        dma((2,)),
        dma((2,)),
    ]
    local_part, turned, halo, weighted, pre = pl.pallas_call(
        functools.partial(exchange, (n_band, n_space, group)),
        out_shape=(
            jax.ShapeDtypeStruct((orbs, cells, cols), F32),
            jax.ShapeDtypeStruct(turned_shape, BF16),
            jax.ShapeDtypeStruct(halo_shape, BF16),
            jax.ShapeDtypeStruct((2, cols, orbs), F32),
            grid_f32,
        ),
        in_specs=[smem, smem, vmem] + [anywhere] * 6,
        out_specs=(anywhere, anywhere, anywhere, vmem, vmem),
        scratch_shapes=scratch,
        compiler_params=pltpu.CompilerParams(
            collective_id=0, has_side_effects=True, vmem_limit_bytes=60 * 1024 * 1024
        ),
    )(
        box_start,
        occupations,
        coupling,
        orbitals,
        potential_in,
        hartree_prev,
        projectors,
        left,
        right,
    )
    return pl.pallas_call(
        functools.partial(apply_terms, n_space),
        out_shape=(jax.ShapeDtypeStruct(orbitals.shape, BF16), grid_f32),
        in_specs=[smem, vmem, vmem, vmem, anywhere, anywhere, anywhere],
        out_specs=(anywhere, vmem),
        scratch_shapes=[
            pltpu.VMEM((orbs, cells, cols), F32),
            pltpu.VMEM(turned_shape, BF16),
            pltpu.VMEM(halo_shape, BF16),
            pltpu.VMEM(orbitals.shape, BF16),
            pltpu.VMEM((2 * atoms * SLOT, cols), BF16),
            pltpu.VMEM((2, cols, wide), F32),
            pltpu.VMEM((rows, 2 * atoms * SLOT, wide), BF16),
            pltpu.VMEM((orbs * cells, cols), F32),
            dma((4,)),
            dma((4,)),
            dma,
            dma((4,)),
        ],
        compiler_params=pltpu.CompilerParams(vmem_limit_bytes=60 * 1024 * 1024),
    )(box_start, weighted, pre, ionic_potential, local_part, turned, halo)


def solution(mesh):
    return jax.shard_map(
        functools.partial(local, mesh.shape["band"], mesh.shape["space"]),
        mesh=mesh,
        in_specs=(
            P("band", "space", None, None),
            P("band"),
            P("space", None, None),
            P("space", None, None),
            P("space", None, None),
            P("space", None, None, None),
            P(),
            P(),
        ),
        out_specs=(P("band", "space", None, None), P("space", None, None)),
        check_vma=False,
    )
```

```python
import functools
import math

import jax
import jax.numpy as jnp
import numpy as np
from jax import lax
from jax.experimental import pallas as pl
from jax.experimental.pallas import tpu as pltpu
from jax.sharding import PartitionSpec as P

SCREENING = 0.25
SWEEPS = 2
FOUR_PI = 4.0 * math.pi
ROWGROUP = 8
MESH = pl.DeviceIdType.MESH
F32 = jnp.float32
BF16 = jnp.bfloat16
SLOT = 16


def stencil_matrices(planes, rows, cols):
    def line(count, periodic):
        matrix = np.zeros((count, count), np.float32)
        for distance, weight in ((1, 16.0), (2, -1.0)):
            for sign in (-1, 1):
                for index in range(count):
                    other = index + sign * distance
                    if periodic:
                        other %= count
                    if 0 <= other < count:
                        matrix[index, other] += weight
        return matrix

    left = np.kron(line(planes, False), np.eye(rows)) + np.kron(np.eye(planes), line(rows, True))
    right = np.kron(np.eye(2), line(cols, True) - 90.0 * np.eye(cols))
    return left.astype(np.float32), right.astype(np.float32)


def tables(box_ref, first_own, first_prev, scat, atoms, cols):
    for part, first in ((0, first_own), (1, first_prev)):
        for a in range(atoms):
            want = lax.broadcasted_iota(jnp.int32, (SLOT, cols), 0) + box_ref[2, first + a]
            zcol = lax.broadcasted_iota(jnp.int32, (SLOT, cols), 1)
            at = (part * atoms + a) * SLOT
            scat[at : at + SLOT, :] = jnp.where(zcol == want, 1.0, 0.0).astype(BF16)


def ownership(orbs, wide, planes):
    lane = lax.broadcasted_iota(jnp.int32, (orbs, wide), 1) // planes
    own = lane == lax.broadcasted_iota(jnp.int32, (orbs, wide), 0)
    return jnp.where(own, 1.0, 0.0).astype(BF16)


def plane_steps(width, wide, planes):
    lane = lax.broadcasted_iota(jnp.int32, (width, wide), 1) % planes
    return lane - lax.broadcasted_iota(jnp.int32, (width, wide), 0)


def exchange(
    dims,
    box_ref,
    occ_ref,
    coup_ref,
    orb_hbm,
    vin_hbm,
    har_hbm,
    proj_hbm,
    left_hbm,
    right_hbm,
    local_part,
    turned,
    halo,
    weighted_out,
    pre_ref,
    orb_ref,
    vin_ref,
    har_ref,
    proj_ref,
    left_ref,
    right_ref,
    pprev,
    hhalo,
    rhalo,
    dens_f,
    dens_b,
    dens_in,
    rho,
    chg1,
    chg2,
    chg3,
    chg_in1,
    chg_in2,
    chg_in3,
    scat,
    fields,
    gathered,
    partial,
    part_own,
    part_prev,
    got_own,
    got_prev,
    couple,
    hone,
    s_load,
    s_proj,
    r_proj,
    s_fwd,
    r_fwd,
    s_across,
    r_across,
    s_last,
    r_last,
    s_halo,
    r_halo,
    s_hh,
    r_hh,
    s_dens,
    r_dens,
    s_c1,
    r_c1,
    s_c2,
    r_c2,
    s_c3,
    r_c3,
    s_rh,
    r_rh,
    s_part,
    r_part,
):
    n_band, n_space, group = dims
    orbs, planes, rows, cols = orb_ref.shape
    atoms, nproj, width, square = proj_ref.shape
    cells = planes * rows
    wide = orbs * planes
    n_far = n_space // group
    share = atoms // n_band

    me_b = lax.axis_index("band")
    me_s = lax.axis_index("space")
    nxt = lax.rem(me_s + 1, n_space)
    prv = lax.rem(me_s + n_space - 1, n_space)
    core = lax.rem(me_b, 2)
    sib = me_b + 1 - 2 * core
    across = lax.rem(me_b + 2, n_band)
    beyond = lax.rem(sib + 2, n_band)
    near = me_s // n_far
    far = lax.rem(me_s, n_far)

    def band_peer(d):
        return (lax.rem(me_b + d, n_band), me_s)

    def near_peer(d):
        return (me_b, lax.rem(near + d, group) * n_far + far)

    def far_peer(d):
        return (me_b, near * n_far + lax.rem(far + d, n_far))

    partners = [(me_b, nxt), (me_b, prv)]
    partners += [band_peer(d) for d in range(1, n_band)]
    partners += [near_peer(d) for d in range(1, group)]
    partners += [far_peer(d) for d in range(1, n_far)]
    barrier = pltpu.get_barrier_semaphore()
    for partner in partners:
        pl.semaphore_signal(barrier, inc=1, device_id=partner, device_id_type=MESH)

    loads = []
    for n, (src, dst) in enumerate(
        (
            (orb_hbm, orb_ref),
            (proj_hbm, proj_ref),
            (left_hbm, left_ref),
            (right_hbm, right_ref),
            (vin_hbm, vin_ref),
            (har_hbm, har_ref),
        )
    ):
        loads.append(pltpu.make_async_copy(src, dst, s_load.at[n]))
        loads[n].start()

    pl.semaphore_wait(barrier, len(partners))

    sent = []

    def send(src, dst, send_sem, recv_sem, device):
        copy = pltpu.make_async_remote_copy(
            src_ref=src,
            dst_ref=dst,
            send_sem=send_sem,
            recv_sem=recv_sem,
            device_id=device,
            device_id_type=MESH,
        )
        copy.start()
        sent.append(copy)

    def arrived(dst, send_sem, recv_sem):
        pltpu.make_async_remote_copy(
            src_ref=dst,
            dst_ref=dst,
            send_sem=send_sem,
            recv_sem=recv_sem,
            device_id=(me_b, nxt),
            device_id_type=MESH,
        ).wait_recv()

    def send_projectors(h):
        a = me_b * share + h
        send(proj_hbm.at[a], pprev.at[a], s_proj.at[h], r_proj.at[h], (me_b, nxt))

    send_projectors(0)
    send(har_hbm.at[pl.ds(0, 2)], hhalo.at[1], s_hh.at[1], r_hh.at[1], (me_b, prv))
    send(har_hbm.at[pl.ds(planes - 2, 2)], hhalo.at[0], s_hh.at[0], r_hh.at[0], (me_b, nxt))
    first_own = me_s * atoms
    first_prev = prv * atoms
    tables(box_ref, first_own, first_prev, scat, atoms, cols)

    loads[0].wait()

    def density_plane(i, charge):
        total = jnp.zeros((rows, cols), F32)
        for o in range(orbs):
            field = orb_ref[o, i].astype(F32)
            at = (o * planes + i) * rows
            fields[pl.ds(pl.multiple_of(at, rows), rows), :] = field
            total = total + (occ_ref[o] * field) * field
        dens_f[i] = total
        dens_b[i] = total.astype(BF16)
        for r in range(0, rows, ROWGROUP):
            charge = charge + total[r : r + ROWGROUP]
        return charge

    chg1[...] = lax.fori_loop(0, planes, density_plane, jnp.zeros((ROWGROUP, cols), F32))
    for d in range(1, group):
        send(chg1, chg_in2.at[near], s_c2.at[d], r_c2.at[near], near_peer(d))
    for h in range(1, share):
        send_projectors(h)
    for d in range(1, n_band):
        send(dens_b, dens_in.at[me_b], s_dens.at[d], r_dens.at[me_b], band_peer(d))

    send(orb_ref.at[:, pl.ds(0, 2)], halo.at[1], s_halo.at[1], r_halo.at[1], (me_b, prv))

    for y in range(rows):
        line = fields[pl.ds(y, wide, stride=rows), :].astype(BF16)
        cut = lax.dot_general(
            scat[...], line, (((1,), (1,)), ((), ())), preferred_element_type=F32
        ).astype(BF16)
        for n in range(2 * atoms):
            gathered[n, y * SLOT : (y + 1) * SLOT, :] = cut[n * SLOT : (n + 1) * SLOT, :]

    belongs = ownership(orbs, wide, planes)
    step = plane_steps(width, wide, planes)

    def gather(part, source, first, a):
        beta = source[a].reshape(nproj * width, square)
        turned[part * atoms + a] = beta.T
        pairs = jnp.dot(beta, gathered[part * atoms + a], preferred_element_type=F32)
        keep = step == lax.rem(box_ref[0, first + a], planes) - part * planes
        pairs = jnp.where(keep[None], pairs.reshape(nproj, width, wide), 0.0)
        folded = pairs[:, :ROWGROUP] + pairs[:, ROWGROUP:]
        folded = folded.reshape(nproj * ROWGROUP, wide)
        at = pl.ds(pl.multiple_of(a * nproj * ROWGROUP, ROWGROUP), nproj * ROWGROUP)
        for t in range(wide // cols):
            partial[t, at, :] = folded[:, t * cols : (t + 1) * cols]

    def gathered_sum():
        count = atoms * nproj
        tiles = []
        for t in range(wide // cols):
            total = partial[t, pl.ds(0, count, stride=ROWGROUP), :]
            for r in range(1, ROWGROUP):
                total = total + partial[t, pl.ds(r, count, stride=ROWGROUP), :]
            tiles.append(total)
        total = jnp.concatenate(tiles, axis=1)
        total = jnp.concatenate([total, jnp.zeros((cols - count, wide), F32)], axis=0)
        high = total.astype(BF16)
        low = (total - high.astype(F32)).astype(BF16)
        lanes = (((1,), (1,)), ((), ()))
        return lax.dot_general(
            belongs, high, lanes, preferred_element_type=F32
        ) + lax.dot_general(belongs, low, lanes, preferred_element_type=F32)

    def hand_on(h):
        a = me_b * share + h
        arrived(pprev.at[a], s_proj.at[h], r_proj.at[h])
        send(pprev.at[a], pprev.at[a], s_across.at[h], r_across.at[h], (across, me_s))
        send(pprev.at[a], pprev.at[a], s_fwd.at[h], r_fwd.at[h], (sib, me_s))

    def hand_across(h):
        a = across * share + h
        arrived(pprev.at[a], s_across.at[h], r_across.at[h])
        send(pprev.at[a], pprev.at[a], s_last.at[h], r_last.at[h], (sib, me_s))

    hand_on(0)
    loads[1].wait()
    for a in range(atoms):
        gather(0, proj_ref, first_own, a)
    part_own[...] = gathered_sum()
    send(part_own, got_prev, s_part.at[0], r_part.at[0], (me_b, nxt))

    hand_on(1)

    for d in range(1, group):
        peer = lax.rem(near + d, group)
        arrived(chg_in2.at[peer], s_c2.at[d], r_c2.at[peer])
    charge = chg1[...]
    for d in range(1, group):
        charge = charge + chg_in2[lax.rem(near + d, group)]
    chg2[...] = charge
    for d in range(1, n_far):
        send(chg2, chg_in3.at[far], s_c3.at[d], r_c3.at[far], far_peer(d))
    send(orb_ref.at[:, pl.ds(planes - 2, 2)], halo.at[0], s_halo.at[0], r_halo.at[0], (me_b, nxt))

    for n in range(2, 5):
        loads[n].wait()
    for pair in range(orbs // 2):
        if pair == orbs // 4:
            hand_across(0)
        first, second = orb_ref[2 * pair], orb_ref[2 * pair + 1]
        both = jnp.concatenate([first.reshape(cells, cols), second.reshape(cells, cols)], axis=1)
        lap = jnp.dot(left_ref[...], both, preferred_element_type=F32)
        lap = lap + jnp.dot(both, right_ref[...], preferred_element_type=F32)
        vin = vin_ref[...].reshape(cells, cols)
        for n in range(2):
            field = both[:, n * cols : (n + 1) * cols].astype(F32)
            local_part[2 * pair + n] = lap[:, n * cols : (n + 1) * cols] * (-0.5 / 12.0) + vin * field
    hand_across(1)

    for d in range(1, n_band):
        peer = lax.rem(me_b + d, n_band)
        arrived(dens_in.at[peer], s_dens.at[d], r_dens.at[peer])
    total_density = dens_f[...]
    for d in range(1, n_band):
        total_density = total_density + dens_in[lax.rem(me_b + d, n_band)].astype(F32)
    rho[...] = total_density
    send(rho.at[0], rhalo.at[1], s_rh.at[1], r_rh.at[1], (me_b, prv))
    send(rho.at[planes - 1], rhalo.at[0], s_rh.at[0], r_rh.at[0], (me_b, nxt))
    for d in range(1, n_far):
        peer = lax.rem(far + d, n_far)
        arrived(chg_in3.at[peer], s_c3.at[d], r_c3.at[peer])
    charge = chg2[...]
    for d in range(1, n_far):
        charge = charge + chg_in3[lax.rem(far + d, n_far)]
    chg3[...] = charge
    for d in range(1, n_band):
        send(chg3, chg_in1.at[me_b], s_c1.at[d], r_c1.at[me_b], band_peer(d))

    for base in (me_b, across):
        for h in range(share):
            gather(1, pprev, first_prev, base * share + h)
    for base, send_sem, recv_sem in ((sib, s_fwd, r_fwd), (beyond, s_last, r_last)):
        for h in range(share):
            a = base * share + h
            arrived(pprev.at[a], send_sem.at[h], recv_sem.at[h])
            gather(1, pprev, first_prev, a)
    part_prev[...] = gathered_sum()
    send(part_prev, got_own, s_part.at[1], r_part.at[1], (me_b, prv))

    loads[5].wait()
    for side in range(2):
        arrived(hhalo.at[side], s_hh.at[side], r_hh.at[side])
        arrived(rhalo.at[side], s_rh.at[side], r_rh.at[side])

    def around(cell):
        return (
            pltpu.roll(cell, 1, 0)
            + pltpu.roll(cell, rows - 1, 0)
            + pltpu.roll(cell, 1, 1)
            + pltpu.roll(cell, cols - 1, 1)
        )

    def start_plane(p):
        if p < 0:
            return hhalo[0, p + 2]
        if p >= planes:
            return hhalo[1, p - planes]
        return har_ref[p]

    def rho_plane(p):
        if p < 0:
            return rhalo[0]
        if p >= planes:
            return rhalo[1]
        return rho[p]

    inverse = 1.0 / (6.0 + SCREENING)
    for p in range(-1, planes + 1):
        total = start_plane(p - 1) + start_plane(p + 1) + around(start_plane(p))
        hone[p + 1] = (total + FOUR_PI * rho_plane(p)) * inverse
    for d in range(1, n_band):
        peer = lax.rem(me_b + d, n_band)
        arrived(chg_in1.at[peer], s_c1.at[d], r_c1.at[peer])
    charge = chg3[...]
    for d in range(1, n_band):
        charge = charge + chg_in1[lax.rem(me_b + d, n_band)]
    mean = jnp.sum(charge, axis=(0, 1), keepdims=True) * (1.0 / (cells * cols * n_space))
    lift = FOUR_PI * inverse * (1.0 + 6.0 * inverse) * mean
    for p in range(planes):
        total = hone[p] + hone[p + 2] + around(hone[p + 1])
        second = (total + FOUR_PI * rho[p]) * inverse
        root = jnp.exp(jnp.log(rho[p] * (3.0 / math.pi)) * (1.0 / 3.0))
        pre_ref[p] = (second - lift) - root

    row_id = lax.broadcasted_iota(jnp.int32, (cols, nproj), 0) % nproj
    pick = jnp.where(
        row_id == lax.broadcasted_iota(jnp.int32, (cols, nproj), 1), 1.0, 0.0
    ).astype(F32)
    tall = jnp.dot(
        pick, coup_ref[...], precision=lax.Precision.HIGHEST, preferred_element_type=F32
    )
    full = lax.dot_general(
        tall,
        pick,
        (((1,), (1,)), ((), ())),
        precision=lax.Precision.HIGHEST,
        preferred_element_type=F32,
    )
    same = (
        lax.broadcasted_iota(jnp.int32, (cols, cols), 0) // nproj
        == lax.broadcasted_iota(jnp.int32, (cols, cols), 1) // nproj
    )
    couple[...] = jnp.where(same, full, 0.0)

    arrived(got_prev, s_part.at[0], r_part.at[0])
    arrived(got_own, s_part.at[1], r_part.at[1])
    for part, mine, other in ((0, part_own, got_own), (1, part_prev, got_prev)):
        weighted_out[part] = lax.dot_general(
            couple[...],
            mine[...] + other[...],
            (((1,), (1,)), ((), ())),
            precision=lax.Precision.HIGHEST,
            preferred_element_type=F32,
        )

    for side in range(2):
        arrived(halo.at[side], s_halo.at[side], r_halo.at[side])
    for copy in sent:
        copy.wait_send()


def apply_terms(
    n_space,
    box_ref,
    weighted_ref,
    pre_ref,
    ion_ref,
    local_part,
    turned,
    halo,
    app_hbm,
    pot_ref,
    app_ref,
    scat,
    weights,
    added,
    nonlocal_part,
    s_app,
):
    orbs, planes, rows, cols = app_ref.shape
    cells = planes * rows
    wide = orbs * planes
    atoms2, square, depth = turned.shape
    atoms = atoms2 // 2
    width = planes
    nproj = depth // width
    me_s = lax.axis_index("space")
    prv = lax.rem(me_s + n_space - 1, n_space)
    firsts = (me_s * atoms, prv * atoms)
    batches = s_app.shape[0]
    some = orbs // batches


    tables(box_ref, firsts[0], firsts[1], scat, atoms, cols)
    belongs = ownership(orbs, wide, planes)
    step = plane_steps(width, wide, planes)
    for part in range(2):
        weights[part] = jnp.dot(
            weighted_ref[part].astype(BF16), belongs, preferred_element_type=F32
        )
    pot_ref[...] = ion_ref[...] + pre_ref[...]
    for n in range(atoms2):
        part, a = n // atoms, n % atoms
        keep = step == lax.rem(box_ref[0, firsts[part] + a], planes) - part * planes
        rows_a = weights[part, a * nproj : (a + 1) * nproj, :].reshape(nproj, 1, wide)
        placed = jnp.where(keep[None], rows_a, 0.0)
        placed = placed.reshape(nproj * width, wide).astype(BF16)
        term = jnp.dot(turned[n], placed, preferred_element_type=F32).astype(BF16)
        for y in range(rows):
            added[y, n * SLOT : (n + 1) * SLOT, :] = term[y * SLOT : (y + 1) * SLOT, :]

    for y in range(rows):
        nonlocal_part[pl.ds(y, wide, stride=rows), :] = lax.dot_general(
            added[y], scat[...], (((0,), (0,)), ((), ())), preferred_element_type=F32
        )

    outs = []
    scale = -0.5 / 12.0
    for n in range(batches):

        def finish(o, carry):
            near_low, far_low = halo[0, o, 1].astype(F32), halo[0, o, 0].astype(F32)
            near_up, far_up = halo[1, o, 0].astype(F32), halo[1, o, 1].astype(F32)
            edge = {
                0: scale * (16.0 * near_low - far_low),
                1: (-scale) * near_low,
                planes - 2: (-scale) * near_up,
                planes - 1: scale * (16.0 * near_up - far_up),
            }
            for i in range(planes):
                at = pl.ds(pl.multiple_of(o * cells + i * rows, rows), rows)
                total = local_part[o, i * rows : (i + 1) * rows, :] + nonlocal_part[at, :]
                if i in edge:
                    total = total + edge[i]
                app_ref[o, i] = total.astype(BF16)
            return carry

        lax.fori_loop(n * some, (n + 1) * some, finish, 0)
        at = pl.ds(n * some, some)
        outs.append(pltpu.make_async_copy(app_ref.at[at], app_hbm.at[at], s_app.at[n]))
        outs[n].start()
    for copy in outs:
        copy.wait()


def local(
    n_band,
    n_space,
    orbitals,
    occupations,
    potential_in,
    ionic_potential,
    hartree_prev,
    projectors,
    box_start,
    coupling,
):
    orbs, planes, rows, cols = orbitals.shape
    atoms, nproj, width, square = projectors.shape
    cells = planes * rows
    wide = orbs * planes
    group = 8 if n_space % 8 == 0 else 2
    n_far = n_space // group
    share = atoms // n_band
    left, right = stencil_matrices(planes, rows, cols)
    left, right = jnp.asarray(left, BF16), jnp.asarray(right, BF16)
    vmem = pl.BlockSpec(memory_space=pltpu.VMEM)
    smem = pl.BlockSpec(memory_space=pltpu.SMEM)
    anywhere = pl.BlockSpec(memory_space=pl.ANY)
    dma = pltpu.SemaphoreType.DMA
    grid_f32 = jax.ShapeDtypeStruct(potential_in.shape, F32)
    halo_shape = (2, orbs, 2, rows, cols)
    turned_shape = (2 * atoms, square, nproj * width)
    scratch = [
        pltpu.VMEM(orbitals.shape, BF16),
        pltpu.VMEM(potential_in.shape, F32),
        pltpu.VMEM(hartree_prev.shape, F32),
        pltpu.VMEM(projectors.shape, BF16),
        pltpu.VMEM(left.shape, BF16),
        pltpu.VMEM(right.shape, BF16),
        pltpu.VMEM(projectors.shape, BF16),
        pltpu.VMEM((2, 2, rows, cols), F32),
        pltpu.VMEM((2, rows, cols), F32),
        pltpu.VMEM((planes, rows, cols), F32),
        pltpu.VMEM((planes, rows, cols), BF16),
        pltpu.VMEM((n_band, planes, rows, cols), BF16),
        pltpu.VMEM((planes, rows, cols), F32),
        pltpu.VMEM((ROWGROUP, cols), F32),
        pltpu.VMEM((ROWGROUP, cols), F32),
        pltpu.VMEM((ROWGROUP, cols), F32),
        pltpu.VMEM((n_band, ROWGROUP, cols), F32),
        pltpu.VMEM((group, ROWGROUP, cols), F32),
        pltpu.VMEM((n_far, ROWGROUP, cols), F32),
        pltpu.VMEM((2 * atoms * SLOT, cols), BF16),
        pltpu.VMEM((orbs * cells, cols), F32),
        pltpu.VMEM((2 * atoms, square, wide), BF16),
        pltpu.VMEM((wide // cols, atoms * nproj * ROWGROUP, cols), F32),
        pltpu.VMEM((orbs, cols), F32),
        pltpu.VMEM((orbs, cols), F32),
        pltpu.VMEM((orbs, cols), F32),
        pltpu.VMEM((orbs, cols), F32),
        pltpu.VMEM((cols, cols), F32),
        pltpu.VMEM((planes + 2, rows, cols), F32),
        dma((6,)),
        dma((share,)),
        dma((share,)),
        dma((share,)),
        dma((share,)),
        dma((share,)),
        dma((share,)),
        dma((share,)),
        dma((share,)),
        dma((2,)),
        dma((2,)),
        dma((2,)),
        dma((2,)),
        dma((n_band,)),
        dma((n_band,)),
        dma((n_band,)),
        dma((n_band,)),
        dma((group,)),
        dma((group,)),
        dma((n_far,)),
        dma((n_far,)),
        dma((2,)),
        dma((2,)),
        dma((2,)),
        dma((2,)),
    ]
    handed = pl.pallas_call(
        functools.partial(exchange, (n_band, n_space, group)),
        out_shape=(
            pltpu.VMEM((orbs, cells, cols), F32),
            pltpu.VMEM(turned_shape, BF16),
            pltpu.VMEM(halo_shape, BF16),
            pltpu.VMEM((2, cols, orbs), F32),
            pltpu.VMEM(potential_in.shape, F32),
        ),
        in_specs=[smem, smem, vmem] + [anywhere] * 6,
        out_specs=(vmem,) * 5,
        scratch_shapes=scratch,
        compiler_params=pltpu.CompilerParams(
            collective_id=0, has_side_effects=True, vmem_limit_bytes=54 * 1024 * 1024
        ),
    )(
        box_start,
        occupations,
        coupling,
        orbitals,
        potential_in,
        hartree_prev,
        projectors,
        left,
        right,
    )
    local_part, turned, halo, weighted, pre = (
        pltpu.with_memory_space_constraint(array, pltpu.VMEM) for array in handed
    )
    return pl.pallas_call(
        functools.partial(apply_terms, n_space),
        out_shape=(jax.ShapeDtypeStruct(orbitals.shape, BF16), grid_f32),
        in_specs=[smem] + [vmem] * 6,
        out_specs=(anywhere, vmem),
        scratch_shapes=[
            pltpu.VMEM(orbitals.shape, BF16),
            pltpu.VMEM((2 * atoms * SLOT, cols), BF16),
            pltpu.VMEM((2, cols, wide), F32),
            pltpu.VMEM((rows, 2 * atoms * SLOT, wide), BF16),
            pltpu.VMEM((orbs * cells, cols), F32),
            dma((4,)),
        ],
        compiler_params=pltpu.CompilerParams(vmem_limit_bytes=54 * 1024 * 1024),
    )(box_start, weighted, pre, ionic_potential, local_part, turned, halo)


def solution(mesh):
    return jax.shard_map(
        functools.partial(local, mesh.shape["band"], mesh.shape["space"]),
        mesh=mesh,
        in_specs=(
            P("band", "space", None, None),
            P("band"),
            P("space", None, None),
            P("space", None, None),
            P("space", None, None),
            P("space", None, None, None),
            P(),
            P(),
        ),
        out_specs=(P("band", "space", None, None), P("space", None, None)),
        check_vma=False,
    )
```

```python
import functools
import math

import jax
import jax.numpy as jnp
import numpy as np
from jax import lax
from jax.experimental import pallas as pl
from jax.experimental.pallas import tpu as pltpu
from jax.sharding import PartitionSpec as P

SCREENING = 0.25
SWEEPS = 2
FOUR_PI = 4.0 * math.pi
ROWGROUP = 8
MESH = pl.DeviceIdType.MESH
F32 = jnp.float32
BF16 = jnp.bfloat16
SLOT = 16


def stencil_matrices(planes, rows, cols):
    def line(count, periodic):
        matrix = np.zeros((count, count), np.float32)
        for distance, weight in ((1, 16.0), (2, -1.0)):
            for sign in (-1, 1):
                for index in range(count):
                    other = index + sign * distance
                    if periodic:
                        other %= count
                    if 0 <= other < count:
                        matrix[index, other] += weight
        return matrix

    left = np.kron(line(planes, False), np.eye(rows)) + np.kron(np.eye(planes), line(rows, True))
    right = np.kron(np.eye(2), line(cols, True) - 90.0 * np.eye(cols))
    return left.astype(np.float32), right.astype(np.float32)


def tables(box_ref, first_own, first_prev, scat, atoms, cols):
    for part, first in ((0, first_own), (1, first_prev)):
        for a in range(atoms):
            want = lax.broadcasted_iota(jnp.int32, (SLOT, cols), 0) + box_ref[2, first + a]
            zcol = lax.broadcasted_iota(jnp.int32, (SLOT, cols), 1)
            at = (part * atoms + a) * SLOT
            scat[at : at + SLOT, :] = jnp.where(zcol == want, 1.0, 0.0).astype(BF16)


def ownership(orbs, wide, planes):
    lane = lax.broadcasted_iota(jnp.int32, (orbs, wide), 1) // planes
    own = lane == lax.broadcasted_iota(jnp.int32, (orbs, wide), 0)
    return jnp.where(own, 1.0, 0.0).astype(BF16)


def plane_steps(width, wide, planes):
    lane = lax.broadcasted_iota(jnp.int32, (width, wide), 1) % planes
    return lane - lax.broadcasted_iota(jnp.int32, (width, wide), 0)


def exchange(
    dims,
    box_ref,
    occ_ref,
    coup_ref,
    orb_hbm,
    vin_hbm,
    har_hbm,
    proj_hbm,
    left_hbm,
    right_hbm,
    local_part,
    fields,
    halo,
    charge_out,
    pre_ref,
    orb_ref,
    vin_ref,
    har_ref,
    proj_ref,
    left_ref,
    right_ref,
    pprev,
    hhalo,
    rhalo,
    dens_f,
    dens_b,
    dens_in,
    rho,
    chg1,
    chg2,
    chg3,
    chg_in1,
    chg_in2,
    chg_in3,
    scat,
    gathered,
    turned,
    partial,
    weights,
    added,
    part_own,
    part_prev,
    got_own,
    got_prev,
    couple,
    hone,
    s_load,
    s_proj,
    r_proj,
    s_fwd,
    r_fwd,
    s_across,
    r_across,
    s_last,
    r_last,
    s_halo,
    r_halo,
    s_hh,
    r_hh,
    s_dens,
    r_dens,
    s_c1,
    r_c1,
    s_c2,
    r_c2,
    s_c3,
    r_c3,
    s_rh,
    r_rh,
    s_part,
    r_part,
):
    n_band, n_space, group = dims
    orbs, planes, rows, cols = orb_ref.shape
    atoms, nproj, width, square = proj_ref.shape
    cells = planes * rows
    wide = orbs * planes
    n_far = n_space // group
    share = atoms // n_band

    me_b = lax.axis_index("band")
    me_s = lax.axis_index("space")
    nxt = lax.rem(me_s + 1, n_space)
    prv = lax.rem(me_s + n_space - 1, n_space)
    core = lax.rem(me_b, 2)
    sib = me_b + 1 - 2 * core
    across = lax.rem(me_b + 2, n_band)
    beyond = lax.rem(sib + 2, n_band)
    near = me_s // n_far
    far = lax.rem(me_s, n_far)

    def band_peer(d):
        return (lax.rem(me_b + d, n_band), me_s)

    def near_peer(d):
        return (me_b, lax.rem(near + d, group) * n_far + far)

    def far_peer(d):
        return (me_b, near * n_far + lax.rem(far + d, n_far))

    partners = [(me_b, nxt), (me_b, prv)]
    partners += [band_peer(d) for d in range(1, n_band)]
    partners += [near_peer(d) for d in range(1, group)]
    partners += [far_peer(d) for d in range(1, n_far)]
    barrier = pltpu.get_barrier_semaphore()
    for partner in partners:
        pl.semaphore_signal(barrier, inc=1, device_id=partner, device_id_type=MESH)

    loads = []
    for n, (src, dst) in enumerate(
        (
            (orb_hbm, orb_ref),
            (proj_hbm, proj_ref),
            (left_hbm, left_ref),
            (right_hbm, right_ref),
            (vin_hbm, vin_ref),
            (har_hbm, har_ref),
        )
    ):
        loads.append(pltpu.make_async_copy(src, dst, s_load.at[n]))
        loads[n].start()

    pl.semaphore_wait(barrier, len(partners))

    sent = []

    def send(src, dst, send_sem, recv_sem, device):
        copy = pltpu.make_async_remote_copy(
            src_ref=src,
            dst_ref=dst,
            send_sem=send_sem,
            recv_sem=recv_sem,
            device_id=device,
            device_id_type=MESH,
        )
        copy.start()
        sent.append(copy)

    def arrived(dst, send_sem, recv_sem):
        pltpu.make_async_remote_copy(
            src_ref=dst,
            dst_ref=dst,
            send_sem=send_sem,
            recv_sem=recv_sem,
            device_id=(me_b, nxt),
            device_id_type=MESH,
        ).wait_recv()

    def send_projectors(h):
        a = me_b * share + h
        send(proj_hbm.at[a], pprev.at[a], s_proj.at[h], r_proj.at[h], (me_b, nxt))

    send_projectors(0)
    send(har_hbm.at[pl.ds(0, 2)], hhalo.at[1], s_hh.at[1], r_hh.at[1], (me_b, prv))
    send(har_hbm.at[pl.ds(planes - 2, 2)], hhalo.at[0], s_hh.at[0], r_hh.at[0], (me_b, nxt))
    first_own = me_s * atoms
    first_prev = prv * atoms
    tables(box_ref, first_own, first_prev, scat, atoms, cols)

    loads[0].wait()

    def density_plane(i, charge):
        total = jnp.zeros((rows, cols), F32)
        for o in range(orbs):
            field = orb_ref[o, i].astype(F32)
            at = (o * planes + i) * rows
            fields[pl.ds(pl.multiple_of(at, rows), rows), :] = field
            total = total + (occ_ref[o] * field) * field
        dens_f[i] = total
        dens_b[i] = total.astype(BF16)
        for r in range(0, rows, ROWGROUP):
            charge = charge + total[r : r + ROWGROUP]
        return charge

    chg1[...] = lax.fori_loop(0, planes, density_plane, jnp.zeros((ROWGROUP, cols), F32))
    for d in range(1, group):
        send(chg1, chg_in2.at[near], s_c2.at[d], r_c2.at[near], near_peer(d))
    for h in range(1, share):
        send_projectors(h)
    for d in range(1, n_band):
        send(dens_b, dens_in.at[me_b], s_dens.at[d], r_dens.at[me_b], band_peer(d))

    send(orb_ref.at[:, pl.ds(0, 2)], halo.at[1], s_halo.at[1], r_halo.at[1], (me_b, prv))

    for y in range(rows):
        line = fields[pl.ds(y, wide, stride=rows), :].astype(BF16)
        cut = lax.dot_general(
            scat[...], line, (((1,), (1,)), ((), ())), preferred_element_type=F32
        ).astype(BF16)
        for n in range(2 * atoms):
            gathered[n, y * SLOT : (y + 1) * SLOT, :] = cut[n * SLOT : (n + 1) * SLOT, :]

    belongs = ownership(orbs, wide, planes)
    step = plane_steps(width, wide, planes)

    def gather(part, source, first, a):
        beta = source[a].reshape(nproj * width, square)
        turned[part * atoms + a] = beta.T
        pairs = jnp.dot(beta, gathered[part * atoms + a], preferred_element_type=F32)
        keep = step == lax.rem(box_ref[0, first + a], planes) - part * planes
        pairs = jnp.where(keep[None], pairs.reshape(nproj, width, wide), 0.0)
        folded = pairs[:, :ROWGROUP] + pairs[:, ROWGROUP:]
        folded = folded.reshape(nproj * ROWGROUP, wide)
        at = pl.ds(pl.multiple_of(a * nproj * ROWGROUP, ROWGROUP), nproj * ROWGROUP)
        for t in range(wide // cols):
            partial[t, at, :] = folded[:, t * cols : (t + 1) * cols]

    def gathered_sum():
        count = atoms * nproj
        tiles = []
        for t in range(wide // cols):
            total = partial[t, pl.ds(0, count, stride=ROWGROUP), :]
            for r in range(1, ROWGROUP):
                total = total + partial[t, pl.ds(r, count, stride=ROWGROUP), :]
            tiles.append(total)
        total = jnp.concatenate(tiles, axis=1)
        total = jnp.concatenate([total, jnp.zeros((cols - count, wide), F32)], axis=0)
        high = total.astype(BF16)
        low = (total - high.astype(F32)).astype(BF16)
        lanes = (((1,), (1,)), ((), ()))
        return lax.dot_general(
            belongs, high, lanes, preferred_element_type=F32
        ) + lax.dot_general(belongs, low, lanes, preferred_element_type=F32)

    def hand_on(h):
        a = me_b * share + h
        arrived(pprev.at[a], s_proj.at[h], r_proj.at[h])
        send(pprev.at[a], pprev.at[a], s_across.at[h], r_across.at[h], (across, me_s))
        send(pprev.at[a], pprev.at[a], s_fwd.at[h], r_fwd.at[h], (sib, me_s))

    def hand_across(h):
        a = across * share + h
        arrived(pprev.at[a], s_across.at[h], r_across.at[h])
        send(pprev.at[a], pprev.at[a], s_last.at[h], r_last.at[h], (sib, me_s))

    hand_on(0)
    loads[1].wait()
    for a in range(atoms):
        gather(0, proj_ref, first_own, a)
    part_own[...] = gathered_sum()
    send(part_own, got_prev, s_part.at[0], r_part.at[0], (me_b, nxt))

    hand_on(1)

    for d in range(1, group):
        peer = lax.rem(near + d, group)
        arrived(chg_in2.at[peer], s_c2.at[d], r_c2.at[peer])
    charge = chg1[...]
    for d in range(1, group):
        charge = charge + chg_in2[lax.rem(near + d, group)]
    chg2[...] = charge
    for d in range(1, n_far):
        send(chg2, chg_in3.at[far], s_c3.at[d], r_c3.at[far], far_peer(d))
    send(orb_ref.at[:, pl.ds(planes - 2, 2)], halo.at[0], s_halo.at[0], r_halo.at[0], (me_b, nxt))

    for n in range(2, 5):
        loads[n].wait()
    for pair in range(orbs // 2):
        if pair == orbs // 4:
            hand_across(0)
        first, second = orb_ref[2 * pair], orb_ref[2 * pair + 1]
        both = jnp.concatenate([first.reshape(cells, cols), second.reshape(cells, cols)], axis=1)
        lap = jnp.dot(left_ref[...], both, preferred_element_type=F32)
        lap = lap + jnp.dot(both, right_ref[...], preferred_element_type=F32)
        vin = vin_ref[...].reshape(cells, cols)
        for n in range(2):
            field = both[:, n * cols : (n + 1) * cols].astype(F32)
            local_part[2 * pair + n] = lap[:, n * cols : (n + 1) * cols] * (-0.5 / 12.0) + vin * field
    hand_across(1)

    for d in range(1, n_band):
        peer = lax.rem(me_b + d, n_band)
        arrived(dens_in.at[peer], s_dens.at[d], r_dens.at[peer])
    total_density = dens_f[...]
    for d in range(1, n_band):
        total_density = total_density + dens_in[lax.rem(me_b + d, n_band)].astype(F32)
    rho[...] = total_density
    send(rho.at[0], rhalo.at[1], s_rh.at[1], r_rh.at[1], (me_b, prv))
    send(rho.at[planes - 1], rhalo.at[0], s_rh.at[0], r_rh.at[0], (me_b, nxt))
    for d in range(1, n_far):
        peer = lax.rem(far + d, n_far)
        arrived(chg_in3.at[peer], s_c3.at[d], r_c3.at[peer])
    charge = chg2[...]
    for d in range(1, n_far):
        charge = charge + chg_in3[lax.rem(far + d, n_far)]
    chg3[...] = charge
    for d in range(1, n_band):
        send(chg3, chg_in1.at[me_b], s_c1.at[d], r_c1.at[me_b], band_peer(d))

    for base in (me_b, across):
        for h in range(share):
            gather(1, pprev, first_prev, base * share + h)
    for base, send_sem, recv_sem in ((sib, s_fwd, r_fwd), (beyond, s_last, r_last)):
        for h in range(share):
            a = base * share + h
            arrived(pprev.at[a], send_sem.at[h], recv_sem.at[h])
            gather(1, pprev, first_prev, a)
    part_prev[...] = gathered_sum()
    send(part_prev, got_own, s_part.at[1], r_part.at[1], (me_b, prv))

    loads[5].wait()
    for side in range(2):
        arrived(hhalo.at[side], s_hh.at[side], r_hh.at[side])
        arrived(rhalo.at[side], s_rh.at[side], r_rh.at[side])

    def around(cell):
        return (
            pltpu.roll(cell, 1, 0)
            + pltpu.roll(cell, rows - 1, 0)
            + pltpu.roll(cell, 1, 1)
            + pltpu.roll(cell, cols - 1, 1)
        )

    def start_plane(p):
        if p < 0:
            return hhalo[0, p + 2]
        if p >= planes:
            return hhalo[1, p - planes]
        return har_ref[p]

    def rho_plane(p):
        if p < 0:
            return rhalo[0]
        if p >= planes:
            return rhalo[1]
        return rho[p]

    inverse = 1.0 / (6.0 + SCREENING)
    for p in range(-1, planes + 1):
        total = start_plane(p - 1) + start_plane(p + 1) + around(start_plane(p))
        hone[p + 1] = (total + FOUR_PI * rho_plane(p)) * inverse
    for p in range(planes):
        total = hone[p] + hone[p + 2] + around(hone[p + 1])
        second = (total + FOUR_PI * rho[p]) * inverse
        root = jnp.exp(jnp.log(rho[p] * (3.0 / math.pi)) * (1.0 / 3.0))
        pre_ref[p] = second - root

    row_id = lax.broadcasted_iota(jnp.int32, (cols, nproj), 0) % nproj
    pick = jnp.where(
        row_id == lax.broadcasted_iota(jnp.int32, (cols, nproj), 1), 1.0, 0.0
    ).astype(F32)
    tall = jnp.dot(
        pick, coup_ref[...], precision=lax.Precision.HIGHEST, preferred_element_type=F32
    )
    full = lax.dot_general(
        tall,
        pick,
        (((1,), (1,)), ((), ())),
        precision=lax.Precision.HIGHEST,
        preferred_element_type=F32,
    )
    same = (
        lax.broadcasted_iota(jnp.int32, (cols, cols), 0) // nproj
        == lax.broadcasted_iota(jnp.int32, (cols, cols), 1) // nproj
    )
    couple[...] = jnp.where(same, full, 0.0)

    arrived(got_prev, s_part.at[0], r_part.at[0])
    arrived(got_own, s_part.at[1], r_part.at[1])
    for part, mine, other in ((0, part_own, got_own), (1, part_prev, got_prev)):
        weighted = lax.dot_general(
            couple[...],
            mine[...] + other[...],
            (((1,), (1,)), ((), ())),
            precision=lax.Precision.HIGHEST,
            preferred_element_type=F32,
        ).astype(BF16)
        weights[part] = jnp.dot(weighted, belongs, preferred_element_type=F32)

    for n in range(2 * atoms):
        part, a = n // atoms, n % atoms
        first = (first_own, first_prev)[part]
        keep = step == lax.rem(box_ref[0, first + a], planes) - part * planes
        rows_a = weights[part, a * nproj : (a + 1) * nproj, :].reshape(nproj, 1, wide)
        placed = jnp.where(keep[None], rows_a, 0.0)
        placed = placed.reshape(nproj * width, wide).astype(BF16)
        term = jnp.dot(turned[n], placed, preferred_element_type=F32).astype(BF16)
        for y in range(rows):
            added[y, n * SLOT : (n + 1) * SLOT, :] = term[y * SLOT : (y + 1) * SLOT, :]
    for y in range(rows):
        fields[pl.ds(y, wide, stride=rows), :] = lax.dot_general(
            added[y], scat[...], (((0,), (0,)), ((), ())), preferred_element_type=F32
        )

    for d in range(1, n_band):
        peer = lax.rem(me_b + d, n_band)
        arrived(chg_in1.at[peer], s_c1.at[d], r_c1.at[peer])
    charge = chg3[...]
    for d in range(1, n_band):
        charge = charge + chg_in1[lax.rem(me_b + d, n_band)]
    charge_out[...] = charge
    for side in range(2):
        arrived(halo.at[side], s_halo.at[side], r_halo.at[side])
    for copy in sent:
        copy.wait_send()


def finish_terms(
    n_space,
    local_part,
    nonlocal_part,
    halo,
    charge_ref,
    pre_ref,
    ion_ref,
    app_hbm,
    pot_ref,
    app_ref,
    s_app,
):
    orbs, planes, rows, cols = app_ref.shape
    cells = planes * rows
    batches = s_app.shape[0]
    some = orbs // batches
    scale = -0.5 / 12.0
    outs = []
    for n in range(batches):
        for o in range(n * some, (n + 1) * some):
            near_low, far_low = halo[0, o, 1].astype(F32), halo[0, o, 0].astype(F32)
            near_up, far_up = halo[1, o, 0].astype(F32), halo[1, o, 1].astype(F32)
            edge = {
                0: scale * (16.0 * near_low - far_low),
                1: (-scale) * near_low,
                planes - 2: (-scale) * near_up,
                planes - 1: scale * (16.0 * near_up - far_up),
            }
            for i in range(planes):
                at = o * cells + i * rows
                total = local_part[o, i * rows : (i + 1) * rows, :]
                total = total + nonlocal_part[at : at + rows, :]
                if i in edge:
                    total = total + edge[i]
                app_ref[o, i] = total.astype(BF16)
        at = pl.ds(n * some, some)
        outs.append(pltpu.make_async_copy(app_ref.at[at], app_hbm.at[at], s_app.at[n]))
        outs[n].start()

    inverse = 1.0 / (6.0 + SCREENING)
    mean = jnp.sum(charge_ref[...], axis=(0, 1), keepdims=True) * (1.0 / (cells * cols * n_space))
    lift = FOUR_PI * inverse * (1.0 + 6.0 * inverse) * mean
    for p in range(planes):
        pot_ref[p] = ion_ref[p] + (pre_ref[p] - lift)
    for copy in outs:
        copy.wait()


def local(
    n_band,
    n_space,
    orbitals,
    occupations,
    potential_in,
    ionic_potential,
    hartree_prev,
    projectors,
    box_start,
    coupling,
):
    orbs, planes, rows, cols = orbitals.shape
    atoms, nproj, width, square = projectors.shape
    cells = planes * rows
    wide = orbs * planes
    group = 8 if n_space % 8 == 0 else 2
    n_far = n_space // group
    share = atoms // n_band
    left, right = stencil_matrices(planes, rows, cols)
    left, right = jnp.asarray(left, BF16), jnp.asarray(right, BF16)
    vmem = pl.BlockSpec(memory_space=pltpu.VMEM)
    smem = pl.BlockSpec(memory_space=pltpu.SMEM)
    anywhere = pl.BlockSpec(memory_space=pl.ANY)
    dma = pltpu.SemaphoreType.DMA
    grid_f32 = jax.ShapeDtypeStruct(potential_in.shape, F32)
    halo_shape = (2, orbs, 2, rows, cols)
    turned_shape = (2 * atoms, square, nproj * width)
    scratch = [
        pltpu.VMEM(orbitals.shape, BF16),
        pltpu.VMEM(potential_in.shape, F32),
        pltpu.VMEM(hartree_prev.shape, F32),
        pltpu.VMEM(projectors.shape, BF16),
        pltpu.VMEM(left.shape, BF16),
        pltpu.VMEM(right.shape, BF16),
        pltpu.VMEM(projectors.shape, BF16),
        pltpu.VMEM((2, 2, rows, cols), F32),
        pltpu.VMEM((2, rows, cols), F32),
        pltpu.VMEM((planes, rows, cols), F32),
        pltpu.VMEM((planes, rows, cols), BF16),
        pltpu.VMEM((n_band, planes, rows, cols), BF16),
        pltpu.VMEM((planes, rows, cols), F32),
        pltpu.VMEM((ROWGROUP, cols), F32),
        pltpu.VMEM((ROWGROUP, cols), F32),
        pltpu.VMEM((ROWGROUP, cols), F32),
        pltpu.VMEM((n_band, ROWGROUP, cols), F32),
        pltpu.VMEM((group, ROWGROUP, cols), F32),
        pltpu.VMEM((n_far, ROWGROUP, cols), F32),
        pltpu.VMEM((2 * atoms * SLOT, cols), BF16),
        pltpu.VMEM((2 * atoms, square, wide), BF16),
        pltpu.VMEM(turned_shape, BF16),
        pltpu.VMEM((wide // cols, atoms * nproj * ROWGROUP, cols), F32),
        pltpu.VMEM((2, cols, wide), F32),
        pltpu.VMEM((rows, 2 * atoms * SLOT, wide), BF16),
        pltpu.VMEM((orbs, cols), F32),
        pltpu.VMEM((orbs, cols), F32),
        pltpu.VMEM((orbs, cols), F32),
        pltpu.VMEM((orbs, cols), F32),
        pltpu.VMEM((cols, cols), F32),
        pltpu.VMEM((planes + 2, rows, cols), F32),
        dma((6,)),
        dma((share,)),
        dma((share,)),
        dma((share,)),
        dma((share,)),
        dma((share,)),
        dma((share,)),
        dma((share,)),
        dma((share,)),
        dma((2,)),
        dma((2,)),
        dma((2,)),
        dma((2,)),
        dma((n_band,)),
        dma((n_band,)),
        dma((n_band,)),
        dma((n_band,)),
        dma((group,)),
        dma((group,)),
        dma((n_far,)),
        dma((n_far,)),
        dma((2,)),
        dma((2,)),
        dma((2,)),
        dma((2,)),
    ]
    handed = pl.pallas_call(
        functools.partial(exchange, (n_band, n_space, group)),
        out_shape=(
            pltpu.VMEM((orbs, cells, cols), F32),
            pltpu.VMEM((orbs * cells, cols), F32),
            pltpu.VMEM(halo_shape, BF16),
            pltpu.VMEM((ROWGROUP, cols), F32),
            pltpu.VMEM(potential_in.shape, F32),
        ),
        in_specs=[smem, smem, vmem] + [anywhere] * 6,
        out_specs=(vmem,) * 5,
        scratch_shapes=scratch,
        compiler_params=pltpu.CompilerParams(
            collective_id=0, has_side_effects=True, vmem_limit_bytes=54 * 1024 * 1024
        ),
    )(
        box_start,
        occupations,
        coupling,
        orbitals,
        potential_in,
        hartree_prev,
        projectors,
        left,
        right,
    )
    handed = [pltpu.with_memory_space_constraint(array, pltpu.VMEM) for array in handed]
    return pl.pallas_call(
        functools.partial(finish_terms, n_space),
        out_shape=(jax.ShapeDtypeStruct(orbitals.shape, BF16), grid_f32),
        in_specs=[vmem] * 6,
        out_specs=(anywhere, vmem),
        scratch_shapes=[pltpu.VMEM(orbitals.shape, BF16), dma((4,))],
        compiler_params=pltpu.CompilerParams(vmem_limit_bytes=54 * 1024 * 1024),
    )(*handed, ionic_potential)


def solution(mesh):
    return jax.shard_map(
        functools.partial(local, mesh.shape["band"], mesh.shape["space"]),
        mesh=mesh,
        in_specs=(
            P("band", "space", None, None),
            P("band"),
            P("space", None, None),
            P("space", None, None),
            P("space", None, None),
            P("space", None, None, None),
            P(),
            P(),
        ),
        out_specs=(P("band", "space", None, None), P("space", None, None)),
        check_vma=False,
    )
```

```python
import functools
import math

import jax
import jax.numpy as jnp
import numpy as np
from jax import lax
from jax.experimental import pallas as pl
from jax.experimental.pallas import tpu as pltpu
from jax.sharding import PartitionSpec as P

SCREENING = 0.25
SWEEPS = 2
FOUR_PI = 4.0 * math.pi
ROWGROUP = 8
MESH = pl.DeviceIdType.MESH
F32 = jnp.float32
BF16 = jnp.bfloat16
SLOT = 16


def stencil_matrices(planes, rows, cols):
    def line(count, periodic):
        matrix = np.zeros((count, count), np.float32)
        for distance, weight in ((1, 16.0), (2, -1.0)):
            for sign in (-1, 1):
                for index in range(count):
                    other = index + sign * distance
                    if periodic:
                        other %= count
                    if 0 <= other < count:
                        matrix[index, other] += weight
        return matrix

    left = np.kron(line(planes, False), np.eye(rows)) + np.kron(np.eye(planes), line(rows, True))
    right = np.kron(np.eye(2), line(cols, True) - 90.0 * np.eye(cols))
    return left.astype(np.float32), right.astype(np.float32)


def tables(box_ref, first_own, first_prev, scat, atoms, cols):
    for part, first in ((0, first_own), (1, first_prev)):
        for a in range(atoms):
            want = lax.broadcasted_iota(jnp.int32, (SLOT, cols), 0) + box_ref[2, first + a]
            zcol = lax.broadcasted_iota(jnp.int32, (SLOT, cols), 1)
            at = (part * atoms + a) * SLOT
            scat[at : at + SLOT, :] = jnp.where(zcol == want, 1.0, 0.0).astype(BF16)


def ownership(orbs, wide, planes):
    lane = lax.broadcasted_iota(jnp.int32, (orbs, wide), 1) // planes
    own = lane == lax.broadcasted_iota(jnp.int32, (orbs, wide), 0)
    return jnp.where(own, 1.0, 0.0).astype(BF16)


def plane_steps(width, wide, planes):
    lane = lax.broadcasted_iota(jnp.int32, (width, wide), 1) % planes
    return lane - lax.broadcasted_iota(jnp.int32, (width, wide), 0)


def exchange(
    dims,
    box_ref,
    occ_ref,
    coup_ref,
    orb_hbm,
    vin_hbm,
    har_hbm,
    proj_hbm,
    left_hbm,
    right_hbm,
    local_part,
    fields,
    halo,
    charge_out,
    pre_ref,
    orb_ref,
    vin_ref,
    har_ref,
    proj_ref,
    left_ref,
    right_ref,
    pprev,
    hhalo,
    rhalo,
    dens_f,
    dens_b,
    dens_in,
    rho,
    chg1,
    chg2,
    chg3,
    chg_in1,
    chg_in2,
    chg_in3,
    scat,
    gathered,
    turned,
    partial,
    weights,
    added,
    part_own,
    part_prev,
    got_own,
    got_prev,
    couple,
    hone,
    s_load,
    s_proj,
    r_proj,
    s_fwd,
    r_fwd,
    s_across,
    r_across,
    s_last,
    r_last,
    s_halo,
    r_halo,
    s_hh,
    r_hh,
    s_dens,
    r_dens,
    s_c1,
    r_c1,
    s_c2,
    r_c2,
    s_c3,
    r_c3,
    s_rh,
    r_rh,
    s_part,
    r_part,
):
    n_band, n_space, group = dims
    orbs, planes, rows, cols = orb_ref.shape
    atoms, nproj, width, square = proj_ref.shape
    cells = planes * rows
    wide = orbs * planes
    n_far = n_space // group
    share = atoms // n_band

    me_b = lax.axis_index("band")
    me_s = lax.axis_index("space")
    nxt = lax.rem(me_s + 1, n_space)
    prv = lax.rem(me_s + n_space - 1, n_space)
    core = lax.rem(me_b, 2)
    sib = me_b + 1 - 2 * core
    across = lax.rem(me_b + 2, n_band)
    beyond = lax.rem(sib + 2, n_band)
    near = me_s // n_far
    far = lax.rem(me_s, n_far)

    def band_peer(d):
        return (lax.rem(me_b + d, n_band), me_s)

    def near_peer(d):
        return (me_b, lax.rem(near + d, group) * n_far + far)

    def far_peer(d):
        return (me_b, near * n_far + lax.rem(far + d, n_far))

    partners = [(me_b, nxt), (me_b, prv)]
    partners += [band_peer(d) for d in range(1, n_band)]
    partners += [near_peer(d) for d in range(1, group)]
    partners += [far_peer(d) for d in range(1, n_far)]
    barrier = pltpu.get_barrier_semaphore()
    for partner in partners:
        pl.semaphore_signal(barrier, inc=1, device_id=partner, device_id_type=MESH)

    loads = []
    for n, (src, dst) in enumerate(
        (
            (orb_hbm, orb_ref),
            (proj_hbm, proj_ref),
            (left_hbm, left_ref),
            (right_hbm, right_ref),
            (vin_hbm, vin_ref),
            (har_hbm, har_ref),
        )
    ):
        loads.append(pltpu.make_async_copy(src, dst, s_load.at[n]))
        loads[n].start()

    pl.semaphore_wait(barrier, len(partners))

    sent = []

    def send(src, dst, send_sem, recv_sem, device):
        copy = pltpu.make_async_remote_copy(
            src_ref=src,
            dst_ref=dst,
            send_sem=send_sem,
            recv_sem=recv_sem,
            device_id=device,
            device_id_type=MESH,
        )
        copy.start()
        sent.append(copy)

    def arrived(dst, send_sem, recv_sem):
        pltpu.make_async_remote_copy(
            src_ref=dst,
            dst_ref=dst,
            send_sem=send_sem,
            recv_sem=recv_sem,
            device_id=(me_b, nxt),
            device_id_type=MESH,
        ).wait_recv()

    def send_projectors(h):
        a = me_b * share + h
        send(proj_hbm.at[a], pprev.at[a], s_proj.at[h], r_proj.at[h], (me_b, nxt))

    send_projectors(0)
    send(har_hbm.at[pl.ds(0, 2)], hhalo.at[1], s_hh.at[1], r_hh.at[1], (me_b, prv))
    send(har_hbm.at[pl.ds(planes - 2, 2)], hhalo.at[0], s_hh.at[0], r_hh.at[0], (me_b, nxt))
    first_own = me_s * atoms
    first_prev = prv * atoms
    tables(box_ref, first_own, first_prev, scat, atoms, cols)

    loads[0].wait()

    def density_plane(i, charge):
        total = jnp.zeros((rows, cols), F32)
        for o in range(orbs):
            field = orb_ref[o, i].astype(F32)
            at = (o * planes + i) * rows
            fields[pl.ds(pl.multiple_of(at, rows), rows), :] = field
            total = total + (occ_ref[o] * field) * field
        dens_f[i] = total
        dens_b[i] = total.astype(BF16)
        for r in range(0, rows, ROWGROUP):
            charge = charge + total[r : r + ROWGROUP]
        return charge

    chg1[...] = lax.fori_loop(0, planes, density_plane, jnp.zeros((ROWGROUP, cols), F32))
    for d in range(1, group):
        send(chg1, chg_in2.at[near], s_c2.at[d], r_c2.at[near], near_peer(d))
    for h in range(1, share):
        send_projectors(h)
    for d in range(1, n_band):
        send(dens_b, dens_in.at[me_b], s_dens.at[d], r_dens.at[me_b], band_peer(d))

    send(orb_ref.at[:, pl.ds(0, 2)], halo.at[1], s_halo.at[1], r_halo.at[1], (me_b, prv))

    for y in range(rows):
        line = fields[pl.ds(y, wide, stride=rows), :].astype(BF16)
        cut = lax.dot_general(
            scat[...], line, (((1,), (1,)), ((), ())), preferred_element_type=F32
        ).astype(BF16)
        for n in range(2 * atoms):
            gathered[n, y * SLOT : (y + 1) * SLOT, :] = cut[n * SLOT : (n + 1) * SLOT, :]

    belongs = ownership(orbs, wide, planes)
    step = plane_steps(width, wide, planes)

    def gather(part, source, first, a):
        beta = source[a].reshape(nproj * width, square)
        turned[part * atoms + a] = beta.T
        pairs = jnp.dot(beta, gathered[part * atoms + a], preferred_element_type=F32)
        keep = step == lax.rem(box_ref[0, first + a], planes) - part * planes
        pairs = jnp.where(keep[None], pairs.reshape(nproj, width, wide), 0.0)
        folded = pairs[:, :ROWGROUP] + pairs[:, ROWGROUP:]
        folded = folded.reshape(nproj * ROWGROUP, wide)
        at = pl.ds(pl.multiple_of(a * nproj * ROWGROUP, ROWGROUP), nproj * ROWGROUP)
        for t in range(wide // cols):
            partial[t, at, :] = folded[:, t * cols : (t + 1) * cols]

    def gathered_sum():
        count = atoms * nproj
        tiles = []
        for t in range(wide // cols):
            total = partial[t, pl.ds(0, count, stride=ROWGROUP), :]
            for r in range(1, ROWGROUP):
                total = total + partial[t, pl.ds(r, count, stride=ROWGROUP), :]
            tiles.append(total)
        total = jnp.concatenate(tiles, axis=1)
        total = jnp.concatenate([total, jnp.zeros((cols - count, wide), F32)], axis=0)
        high = total.astype(BF16)
        low = (total - high.astype(F32)).astype(BF16)
        lanes = (((1,), (1,)), ((), ()))
        return lax.dot_general(
            belongs, high, lanes, preferred_element_type=F32
        ) + lax.dot_general(belongs, low, lanes, preferred_element_type=F32)

    def hand_on(h):
        a = me_b * share + h
        arrived(pprev.at[a], s_proj.at[h], r_proj.at[h])
        send(pprev.at[a], pprev.at[a], s_across.at[h], r_across.at[h], (across, me_s))
        send(pprev.at[a], pprev.at[a], s_fwd.at[h], r_fwd.at[h], (sib, me_s))

    def hand_across(h):
        a = across * share + h
        arrived(pprev.at[a], s_across.at[h], r_across.at[h])
        send(pprev.at[a], pprev.at[a], s_last.at[h], r_last.at[h], (sib, me_s))

    hand_on(0)
    loads[1].wait()
    for a in range(atoms):
        gather(0, proj_ref, first_own, a)
    part_own[...] = gathered_sum()
    send(part_own, got_prev, s_part.at[0], r_part.at[0], (me_b, nxt))

    hand_on(1)

    for d in range(1, group):
        peer = lax.rem(near + d, group)
        arrived(chg_in2.at[peer], s_c2.at[d], r_c2.at[peer])
    charge = chg1[...]
    for d in range(1, group):
        charge = charge + chg_in2[lax.rem(near + d, group)]
    chg2[...] = charge
    for d in range(1, n_far):
        send(chg2, chg_in3.at[far], s_c3.at[d], r_c3.at[far], far_peer(d))
    send(orb_ref.at[:, pl.ds(planes - 2, 2)], halo.at[0], s_halo.at[0], r_halo.at[0], (me_b, nxt))

    for n in range(2, 5):
        loads[n].wait()
    for pair in range(orbs // 2):
        if pair == orbs // 4:
            hand_across(0)
        first, second = orb_ref[2 * pair], orb_ref[2 * pair + 1]
        both = jnp.concatenate([first.reshape(cells, cols), second.reshape(cells, cols)], axis=1)
        lap = jnp.dot(left_ref[...], both, preferred_element_type=F32)
        lap = lap + jnp.dot(both, right_ref[...], preferred_element_type=F32)
        vin = vin_ref[...].reshape(cells, cols)
        for n in range(2):
            field = both[:, n * cols : (n + 1) * cols].astype(F32)
            local_part[2 * pair + n] = lap[:, n * cols : (n + 1) * cols] * (-0.5 / 12.0) + vin * field
    hand_across(1)

    for d in range(1, n_band):
        peer = lax.rem(me_b + d, n_band)
        arrived(dens_in.at[peer], s_dens.at[d], r_dens.at[peer])
    total_density = dens_f[...]
    for d in range(1, n_band):
        total_density = total_density + dens_in[lax.rem(me_b + d, n_band)].astype(F32)
    rho[...] = total_density
    send(rho.at[0], rhalo.at[1], s_rh.at[1], r_rh.at[1], (me_b, prv))
    send(rho.at[planes - 1], rhalo.at[0], s_rh.at[0], r_rh.at[0], (me_b, nxt))
    for d in range(1, n_far):
        peer = lax.rem(far + d, n_far)
        arrived(chg_in3.at[peer], s_c3.at[d], r_c3.at[peer])
    charge = chg2[...]
    for d in range(1, n_far):
        charge = charge + chg_in3[lax.rem(far + d, n_far)]
    chg3[...] = charge
    for d in range(1, n_band):
        send(chg3, chg_in1.at[me_b], s_c1.at[d], r_c1.at[me_b], band_peer(d))

    for base in (me_b, across):
        for h in range(share):
            gather(1, pprev, first_prev, base * share + h)
    for base, send_sem, recv_sem in ((sib, s_fwd, r_fwd), (beyond, s_last, r_last)):
        for h in range(share):
            a = base * share + h
            arrived(pprev.at[a], send_sem.at[h], recv_sem.at[h])
            gather(1, pprev, first_prev, a)
    part_prev[...] = gathered_sum()
    send(part_prev, got_own, s_part.at[1], r_part.at[1], (me_b, prv))

    loads[5].wait()
    for side in range(2):
        arrived(hhalo.at[side], s_hh.at[side], r_hh.at[side])
        arrived(rhalo.at[side], s_rh.at[side], r_rh.at[side])

    def around(cell):
        return (
            pltpu.roll(cell, 1, 0)
            + pltpu.roll(cell, rows - 1, 0)
            + pltpu.roll(cell, 1, 1)
            + pltpu.roll(cell, cols - 1, 1)
        )

    def start_plane(p):
        if p < 0:
            return hhalo[0, p + 2]
        if p >= planes:
            return hhalo[1, p - planes]
        return har_ref[p]

    def rho_plane(p):
        if p < 0:
            return rhalo[0]
        if p >= planes:
            return rhalo[1]
        return rho[p]

    inverse = 1.0 / (6.0 + SCREENING)
    for p in range(-1, planes + 1):
        total = start_plane(p - 1) + start_plane(p + 1) + around(start_plane(p))
        hone[p + 1] = (total + FOUR_PI * rho_plane(p)) * inverse
    for p in range(planes):
        total = hone[p] + hone[p + 2] + around(hone[p + 1])
        second = (total + FOUR_PI * rho[p]) * inverse
        root = jnp.exp(jnp.log(rho[p] * (3.0 / math.pi)) * (1.0 / 3.0))
        pre_ref[p] = second - root

    row_id = lax.broadcasted_iota(jnp.int32, (cols, nproj), 0) % nproj
    pick = jnp.where(
        row_id == lax.broadcasted_iota(jnp.int32, (cols, nproj), 1), 1.0, 0.0
    ).astype(F32)
    tall = jnp.dot(
        pick, coup_ref[...], precision=lax.Precision.HIGHEST, preferred_element_type=F32
    )
    full = lax.dot_general(
        tall,
        pick,
        (((1,), (1,)), ((), ())),
        precision=lax.Precision.HIGHEST,
        preferred_element_type=F32,
    )
    same = (
        lax.broadcasted_iota(jnp.int32, (cols, cols), 0) // nproj
        == lax.broadcasted_iota(jnp.int32, (cols, cols), 1) // nproj
    )
    couple[...] = jnp.where(same, full, 0.0)

    arrived(got_prev, s_part.at[0], r_part.at[0])
    arrived(got_own, s_part.at[1], r_part.at[1])
    for part, mine, other in ((0, part_own, got_own), (1, part_prev, got_prev)):
        weighted = lax.dot_general(
            couple[...],
            mine[...] + other[...],
            (((1,), (1,)), ((), ())),
            precision=lax.Precision.HIGHEST,
            preferred_element_type=F32,
        ).astype(BF16)
        weights[part] = jnp.dot(weighted, belongs, preferred_element_type=F32)

    for n in range(2 * atoms):
        part, a = n // atoms, n % atoms
        first = (first_own, first_prev)[part]
        keep = step == lax.rem(box_ref[0, first + a], planes) - part * planes
        rows_a = weights[part, a * nproj : (a + 1) * nproj, :].reshape(nproj, 1, wide)
        placed = jnp.where(keep[None], rows_a, 0.0)
        placed = placed.reshape(nproj * width, wide).astype(BF16)
        term = jnp.dot(turned[n], placed, preferred_element_type=F32).astype(BF16)
        for y in range(rows):
            added[y, n * SLOT : (n + 1) * SLOT, :] = term[y * SLOT : (y + 1) * SLOT, :]
    for y in range(rows):
        fields[pl.ds(y, wide, stride=rows), :] = lax.dot_general(
            added[y], scat[...], (((0,), (0,)), ((), ())), preferred_element_type=F32
        )

    for d in range(1, n_band):
        peer = lax.rem(me_b + d, n_band)
        arrived(chg_in1.at[peer], s_c1.at[d], r_c1.at[peer])
    charge = chg3[...]
    for d in range(1, n_band):
        charge = charge + chg_in1[lax.rem(me_b + d, n_band)]
    charge_out[...] = charge
    for side in range(2):
        arrived(halo.at[side], s_halo.at[side], r_halo.at[side])
    for copy in sent:
        copy.wait_send()


def finish_terms(
    n_space,
    local_part,
    nonlocal_part,
    halo,
    charge_ref,
    pre_ref,
    ion_hbm,
    app_hbm,
    pot_hbm,
    app_ref,
    ion_ref,
    pot_ref,
    s_app,
    s_pot,
):
    orbs, planes, rows, cols = app_ref.shape
    cells = planes * rows
    batches = s_app.shape[0]
    some = orbs // batches
    scale = -0.5 / 12.0
    load = pltpu.make_async_copy(ion_hbm, ion_ref, s_pot.at[0])
    load.start()
    outs = []
    for n in range(batches):
        if n == batches // 2:
            inverse = 1.0 / (6.0 + SCREENING)
            total = jnp.sum(charge_ref[...], axis=(0, 1), keepdims=True)
            mean = total * (1.0 / (cells * cols * n_space))
            lift = FOUR_PI * inverse * (1.0 + 6.0 * inverse) * mean
            load.wait()
            for p in range(planes):
                pot_ref[p] = ion_ref[p] + (pre_ref[p] - lift)
            outs.append(pltpu.make_async_copy(pot_ref, pot_hbm, s_pot.at[1]))
            outs[-1].start()
        for o in range(n * some, (n + 1) * some):
            near_low, far_low = halo[0, o, 1].astype(F32), halo[0, o, 0].astype(F32)
            near_up, far_up = halo[1, o, 0].astype(F32), halo[1, o, 1].astype(F32)
            edge = {
                0: scale * (16.0 * near_low - far_low),
                1: (-scale) * near_low,
                planes - 2: (-scale) * near_up,
                planes - 1: scale * (16.0 * near_up - far_up),
            }
            for i in range(planes):
                at = o * cells + i * rows
                total = local_part[o, i * rows : (i + 1) * rows, :]
                total = total + nonlocal_part[at : at + rows, :]
                if i in edge:
                    total = total + edge[i]
                app_ref[o, i] = total.astype(BF16)
        at = pl.ds(n * some, some)
        outs.append(pltpu.make_async_copy(app_ref.at[at], app_hbm.at[at], s_app.at[n]))
        outs[-1].start()
    for copy in outs:
        copy.wait()


def local(
    n_band,
    n_space,
    orbitals,
    occupations,
    potential_in,
    ionic_potential,
    hartree_prev,
    projectors,
    box_start,
    coupling,
):
    orbs, planes, rows, cols = orbitals.shape
    atoms, nproj, width, square = projectors.shape
    cells = planes * rows
    wide = orbs * planes
    group = 8 if n_space % 8 == 0 else 2
    n_far = n_space // group
    share = atoms // n_band
    left, right = stencil_matrices(planes, rows, cols)
    left, right = jnp.asarray(left, BF16), jnp.asarray(right, BF16)
    vmem = pl.BlockSpec(memory_space=pltpu.VMEM)
    smem = pl.BlockSpec(memory_space=pltpu.SMEM)
    anywhere = pl.BlockSpec(memory_space=pl.ANY)
    dma = pltpu.SemaphoreType.DMA
    grid_f32 = jax.ShapeDtypeStruct(potential_in.shape, F32)
    halo_shape = (2, orbs, 2, rows, cols)
    turned_shape = (2 * atoms, square, nproj * width)
    scratch = [
        pltpu.VMEM(orbitals.shape, BF16),
        pltpu.VMEM(potential_in.shape, F32),
        pltpu.VMEM(hartree_prev.shape, F32),
        pltpu.VMEM(projectors.shape, BF16),
        pltpu.VMEM(left.shape, BF16),
        pltpu.VMEM(right.shape, BF16),
        pltpu.VMEM(projectors.shape, BF16),
        pltpu.VMEM((2, 2, rows, cols), F32),
        pltpu.VMEM((2, rows, cols), F32),
        pltpu.VMEM((planes, rows, cols), F32),
        pltpu.VMEM((planes, rows, cols), BF16),
        pltpu.VMEM((n_band, planes, rows, cols), BF16),
        pltpu.VMEM((planes, rows, cols), F32),
        pltpu.VMEM((ROWGROUP, cols), F32),
        pltpu.VMEM((ROWGROUP, cols), F32),
        pltpu.VMEM((ROWGROUP, cols), F32),
        pltpu.VMEM((n_band, ROWGROUP, cols), F32),
        pltpu.VMEM((group, ROWGROUP, cols), F32),
        pltpu.VMEM((n_far, ROWGROUP, cols), F32),
        pltpu.VMEM((2 * atoms * SLOT, cols), BF16),
        pltpu.VMEM((2 * atoms, square, wide), BF16),
        pltpu.VMEM(turned_shape, BF16),
        pltpu.VMEM((wide // cols, atoms * nproj * ROWGROUP, cols), F32),
        pltpu.VMEM((2, cols, wide), F32),
        pltpu.VMEM((rows, 2 * atoms * SLOT, wide), BF16),
        pltpu.VMEM((orbs, cols), F32),
        pltpu.VMEM((orbs, cols), F32),
        pltpu.VMEM((orbs, cols), F32),
        pltpu.VMEM((orbs, cols), F32),
        pltpu.VMEM((cols, cols), F32),
        pltpu.VMEM((planes + 2, rows, cols), F32),
        dma((6,)),
        dma((share,)),
        dma((share,)),
        dma((share,)),
        dma((share,)),
        dma((share,)),
        dma((share,)),
        dma((share,)),
        dma((share,)),
        dma((2,)),
        dma((2,)),
        dma((2,)),
        dma((2,)),
        dma((n_band,)),
        dma((n_band,)),
        dma((n_band,)),
        dma((n_band,)),
        dma((group,)),
        dma((group,)),
        dma((n_far,)),
        dma((n_far,)),
        dma((2,)),
        dma((2,)),
        dma((2,)),
        dma((2,)),
    ]
    handed = pl.pallas_call(
        functools.partial(exchange, (n_band, n_space, group)),
        out_shape=(
            pltpu.VMEM((orbs, cells, cols), F32),
            pltpu.VMEM((orbs * cells, cols), F32),
            pltpu.VMEM(halo_shape, BF16),
            pltpu.VMEM((ROWGROUP, cols), F32),
            pltpu.VMEM(potential_in.shape, F32),
        ),
        in_specs=[smem, smem, vmem] + [anywhere] * 6,
        out_specs=(vmem,) * 5,
        scratch_shapes=scratch,
        compiler_params=pltpu.CompilerParams(
            collective_id=0, has_side_effects=True, vmem_limit_bytes=54 * 1024 * 1024
        ),
    )(
        box_start,
        occupations,
        coupling,
        orbitals,
        potential_in,
        hartree_prev,
        projectors,
        left,
        right,
    )
    handed = [pltpu.with_memory_space_constraint(array, pltpu.VMEM) for array in handed]
    return pl.pallas_call(
        functools.partial(finish_terms, n_space),
        out_shape=(jax.ShapeDtypeStruct(orbitals.shape, BF16), grid_f32),
        in_specs=[vmem] * 5 + [anywhere],
        out_specs=(anywhere, anywhere),
        scratch_shapes=[
            pltpu.VMEM(orbitals.shape, BF16),
            pltpu.VMEM(potential_in.shape, F32),
            pltpu.VMEM(potential_in.shape, F32),
            dma((6,)),
            dma((2,)),
        ],
        compiler_params=pltpu.CompilerParams(vmem_limit_bytes=54 * 1024 * 1024),
    )(*handed, ionic_potential)


def solution(mesh):
    return jax.shard_map(
        functools.partial(local, mesh.shape["band"], mesh.shape["space"]),
        mesh=mesh,
        in_specs=(
            P("band", "space", None, None),
            P("band"),
            P("space", None, None),
            P("space", None, None),
            P("space", None, None),
            P("space", None, None, None),
            P(),
            P(),
        ),
        out_specs=(P("band", "space", None, None), P("space", None, None)),
        check_vma=False,
    )
```

```python
import functools
import math

import jax
import jax.numpy as jnp
import numpy as np
from jax import lax
from jax.experimental import pallas as pl
from jax.experimental.pallas import tpu as pltpu
from jax.sharding import PartitionSpec as P

SCREENING = 0.25
SWEEPS = 2
FOUR_PI = 4.0 * math.pi
ROWGROUP = 8
MESH = pl.DeviceIdType.MESH
F32 = jnp.float32
BF16 = jnp.bfloat16
SLOT = 16


def stencil_matrices(planes, rows, cols):
    def line(count, periodic):
        matrix = np.zeros((count, count), np.float32)
        for distance, weight in ((1, 16.0), (2, -1.0)):
            for sign in (-1, 1):
                for index in range(count):
                    other = index + sign * distance
                    if periodic:
                        other %= count
                    if 0 <= other < count:
                        matrix[index, other] += weight
        return matrix

    left = np.kron(line(planes, False), np.eye(rows)) + np.kron(np.eye(planes), line(rows, True))
    right = np.kron(np.eye(2), line(cols, True) - 90.0 * np.eye(cols))
    return left.astype(np.float32), right.astype(np.float32)


def tables(box_ref, first_own, first_prev, scat, atoms, cols):
    for part, first in ((0, first_own), (1, first_prev)):
        for a in range(atoms):
            want = lax.broadcasted_iota(jnp.int32, (SLOT, cols), 0) + box_ref[2, first + a]
            zcol = lax.broadcasted_iota(jnp.int32, (SLOT, cols), 1)
            at = (part * atoms + a) * SLOT
            scat[at : at + SLOT, :] = jnp.where(zcol == want, 1.0, 0.0).astype(BF16)


def ownership(orbs, wide, planes):
    lane = lax.broadcasted_iota(jnp.int32, (orbs, wide), 1) // planes
    own = lane == lax.broadcasted_iota(jnp.int32, (orbs, wide), 0)
    return jnp.where(own, 1.0, 0.0).astype(BF16)


def plane_steps(width, wide, planes):
    lane = lax.broadcasted_iota(jnp.int32, (width, wide), 1) % planes
    return lane - lax.broadcasted_iota(jnp.int32, (width, wide), 0)


def exchange(
    dims,
    box_ref,
    occ_ref,
    coup_ref,
    orb_hbm,
    vin_hbm,
    har_hbm,
    proj_hbm,
    left_hbm,
    right_hbm,
    local_part,
    fields,
    halo,
    charge_out,
    pre_ref,
    orb_ref,
    vin_ref,
    har_ref,
    proj_ref,
    left_ref,
    right_ref,
    pprev,
    hhalo,
    rhalo,
    dens_f,
    dens_b,
    dens_in,
    rho,
    chg1,
    chg2,
    chg3,
    chg_in1,
    chg_in2,
    chg_in3,
    scat,
    gathered,
    turned,
    partial,
    weights,
    added,
    part_own,
    part_prev,
    got_own,
    got_prev,
    couple,
    hone,
    s_load,
    s_proj,
    r_proj,
    s_fwd,
    r_fwd,
    s_across,
    r_across,
    s_last,
    r_last,
    s_halo,
    r_halo,
    s_hh,
    r_hh,
    s_dens,
    r_dens,
    s_c1,
    r_c1,
    s_c2,
    r_c2,
    s_c3,
    r_c3,
    s_rh,
    r_rh,
    s_part,
    r_part,
):
    n_band, n_space, group = dims
    orbs, planes, rows, cols = orb_ref.shape
    atoms, nproj, width, square = proj_ref.shape
    cells = planes * rows
    wide = orbs * planes
    n_far = n_space // group
    share = atoms // n_band

    me_b = lax.axis_index("band")
    me_s = lax.axis_index("space")
    nxt = lax.rem(me_s + 1, n_space)
    prv = lax.rem(me_s + n_space - 1, n_space)
    core = lax.rem(me_b, 2)
    sib = me_b + 1 - 2 * core
    across = lax.rem(me_b + 2, n_band)
    beyond = lax.rem(sib + 2, n_band)
    near = me_s // n_far
    far = lax.rem(me_s, n_far)

    def band_peer(d):
        return (lax.rem(me_b + d, n_band), me_s)

    def near_peer(d):
        return (me_b, lax.rem(near + d, group) * n_far + far)

    def far_peer(d):
        return (me_b, near * n_far + lax.rem(far + d, n_far))

    partners = [(me_b, nxt), (me_b, prv)]
    partners += [band_peer(d) for d in range(1, n_band)]
    partners += [near_peer(d) for d in range(1, group)]
    partners += [far_peer(d) for d in range(1, n_far)]
    barrier = pltpu.get_barrier_semaphore()
    for partner in partners:
        pl.semaphore_signal(barrier, inc=1, device_id=partner, device_id_type=MESH)

    loads = []
    for n, (src, dst) in enumerate(
        (
            (orb_hbm, orb_ref),
            (proj_hbm, proj_ref),
            (left_hbm, left_ref),
            (right_hbm, right_ref),
            (vin_hbm, vin_ref),
            (har_hbm, har_ref),
        )
    ):
        loads.append(pltpu.make_async_copy(src, dst, s_load.at[n]))
        loads[n].start()

    pl.semaphore_wait(barrier, len(partners))

    sent = []

    def send(src, dst, send_sem, recv_sem, device):
        copy = pltpu.make_async_remote_copy(
            src_ref=src,
            dst_ref=dst,
            send_sem=send_sem,
            recv_sem=recv_sem,
            device_id=device,
            device_id_type=MESH,
        )
        copy.start()
        sent.append(copy)

    def arrived(dst, send_sem, recv_sem):
        pltpu.make_async_remote_copy(
            src_ref=dst,
            dst_ref=dst,
            send_sem=send_sem,
            recv_sem=recv_sem,
            device_id=(me_b, nxt),
            device_id_type=MESH,
        ).wait_recv()

    def send_projectors(h):
        a = me_b * share + h
        send(proj_hbm.at[a], pprev.at[a], s_proj.at[h], r_proj.at[h], (me_b, nxt))

    send_projectors(0)
    send(har_hbm.at[pl.ds(0, 2)], hhalo.at[1], s_hh.at[1], r_hh.at[1], (me_b, prv))
    send(har_hbm.at[pl.ds(planes - 2, 2)], hhalo.at[0], s_hh.at[0], r_hh.at[0], (me_b, nxt))
    first_own = me_s * atoms
    first_prev = prv * atoms
    tables(box_ref, first_own, first_prev, scat, atoms, cols)

    loads[0].wait()

    def density_plane(i, charge):
        total = jnp.zeros((rows, cols), F32)
        for o in range(orbs):
            field = orb_ref[o, i].astype(F32)
            at = (o * planes + i) * rows
            fields[pl.ds(pl.multiple_of(at, rows), rows), :] = field
            total = total + (occ_ref[o] * field) * field
        dens_f[i] = total
        dens_b[i] = total.astype(BF16)
        for r in range(0, rows, ROWGROUP):
            charge = charge + total[r : r + ROWGROUP]
        return charge

    chg1[...] = lax.fori_loop(0, planes, density_plane, jnp.zeros((ROWGROUP, cols), F32))
    for d in range(1, group):
        send(chg1, chg_in2.at[near], s_c2.at[d], r_c2.at[near], near_peer(d))
    for h in range(1, share):
        send_projectors(h)
    for d in range(1, n_band):
        send(dens_b, dens_in.at[me_b], s_dens.at[d], r_dens.at[me_b], band_peer(d))

    send(orb_ref.at[:, pl.ds(0, 2)], halo.at[1], s_halo.at[1], r_halo.at[1], (me_b, prv))

    for y in range(rows):
        line = fields[pl.ds(y, wide, stride=rows), :].astype(BF16)
        cut = lax.dot_general(
            scat[...], line, (((1,), (1,)), ((), ())), preferred_element_type=F32
        ).astype(BF16)
        for n in range(2 * atoms):
            gathered[n, y * SLOT : (y + 1) * SLOT, :] = cut[n * SLOT : (n + 1) * SLOT, :]

    belongs = ownership(orbs, wide, planes)
    step = plane_steps(width, wide, planes)

    def gather(part, source, first, a):
        beta = source[a].reshape(nproj * width, square)
        turned[part * atoms + a] = beta.T
        pairs = jnp.dot(beta, gathered[part * atoms + a], preferred_element_type=F32)
        keep = step == lax.rem(box_ref[0, first + a], planes) - part * planes
        pairs = jnp.where(keep[None], pairs.reshape(nproj, width, wide), 0.0)
        folded = pairs[:, :ROWGROUP] + pairs[:, ROWGROUP:]
        folded = folded.reshape(nproj * ROWGROUP, wide)
        at = pl.ds(pl.multiple_of(a * nproj * ROWGROUP, ROWGROUP), nproj * ROWGROUP)
        for t in range(wide // cols):
            partial[t, at, :] = folded[:, t * cols : (t + 1) * cols]

    def gathered_sum():
        count = atoms * nproj
        tiles = []
        for t in range(wide // cols):
            total = partial[t, pl.ds(0, count, stride=ROWGROUP), :]
            for r in range(1, ROWGROUP):
                total = total + partial[t, pl.ds(r, count, stride=ROWGROUP), :]
            tiles.append(total)
        total = jnp.concatenate(tiles, axis=1)
        total = jnp.concatenate([total, jnp.zeros((cols - count, wide), F32)], axis=0)
        high = total.astype(BF16)
        low = (total - high.astype(F32)).astype(BF16)
        lanes = (((1,), (1,)), ((), ()))
        return lax.dot_general(
            belongs, high, lanes, preferred_element_type=F32
        ) + lax.dot_general(belongs, low, lanes, preferred_element_type=F32)

    def hand_on(h):
        a = me_b * share + h
        arrived(pprev.at[a], s_proj.at[h], r_proj.at[h])
        send(pprev.at[a], pprev.at[a], s_across.at[h], r_across.at[h], (across, me_s))
        send(pprev.at[a], pprev.at[a], s_fwd.at[h], r_fwd.at[h], (sib, me_s))

    def hand_across(h):
        a = across * share + h
        arrived(pprev.at[a], s_across.at[h], r_across.at[h])
        send(pprev.at[a], pprev.at[a], s_last.at[h], r_last.at[h], (sib, me_s))

    hand_on(0)
    loads[1].wait()
    for a in range(atoms):
        gather(0, proj_ref, first_own, a)
    part_own[...] = gathered_sum()
    send(part_own, got_prev, s_part.at[0], r_part.at[0], (me_b, nxt))

    hand_on(1)

    row_id = lax.broadcasted_iota(jnp.int32, (cols, nproj), 0) % nproj
    pick = jnp.where(
        row_id == lax.broadcasted_iota(jnp.int32, (cols, nproj), 1), 1.0, 0.0
    ).astype(F32)
    tall = jnp.dot(
        pick, coup_ref[...], precision=lax.Precision.HIGHEST, preferred_element_type=F32
    )
    full = lax.dot_general(
        tall,
        pick,
        (((1,), (1,)), ((), ())),
        precision=lax.Precision.HIGHEST,
        preferred_element_type=F32,
    )
    same = (
        lax.broadcasted_iota(jnp.int32, (cols, cols), 0) // nproj
        == lax.broadcasted_iota(jnp.int32, (cols, cols), 1) // nproj
    )
    couple[...] = jnp.where(same, full, 0.0)

    for d in range(1, group):
        peer = lax.rem(near + d, group)
        arrived(chg_in2.at[peer], s_c2.at[d], r_c2.at[peer])
    charge = chg1[...]
    for d in range(1, group):
        charge = charge + chg_in2[lax.rem(near + d, group)]
    chg2[...] = charge
    for d in range(1, n_far):
        send(chg2, chg_in3.at[far], s_c3.at[d], r_c3.at[far], far_peer(d))
    send(orb_ref.at[:, pl.ds(planes - 2, 2)], halo.at[0], s_halo.at[0], r_halo.at[0], (me_b, nxt))

    for h in range(share):
        gather(1, pprev, first_prev, me_b * share + h)

    for n in range(2, 5):
        loads[n].wait()
    for pair in range(orbs // 2):
        if pair == orbs // 4:
            hand_across(0)
        first, second = orb_ref[2 * pair], orb_ref[2 * pair + 1]
        both = jnp.concatenate([first.reshape(cells, cols), second.reshape(cells, cols)], axis=1)
        lap = jnp.dot(left_ref[...], both, preferred_element_type=F32)
        lap = lap + jnp.dot(both, right_ref[...], preferred_element_type=F32)
        vin = vin_ref[...].reshape(cells, cols)
        for n in range(2):
            field = both[:, n * cols : (n + 1) * cols].astype(F32)
            local_part[2 * pair + n] = lap[:, n * cols : (n + 1) * cols] * (-0.5 / 12.0) + vin * field
    hand_across(1)
    for h in range(share):
        gather(1, pprev, first_prev, across * share + h)

    for d in range(1, n_band):
        peer = lax.rem(me_b + d, n_band)
        arrived(dens_in.at[peer], s_dens.at[d], r_dens.at[peer])
    total_density = dens_f[...]
    for d in range(1, n_band):
        total_density = total_density + dens_in[lax.rem(me_b + d, n_band)].astype(F32)
    rho[...] = total_density
    send(rho.at[0], rhalo.at[1], s_rh.at[1], r_rh.at[1], (me_b, prv))
    send(rho.at[planes - 1], rhalo.at[0], s_rh.at[0], r_rh.at[0], (me_b, nxt))
    for base, send_sem, recv_sem in ((sib, s_fwd, r_fwd), (beyond, s_last, r_last)):
        for h in range(share):
            a = base * share + h
            arrived(pprev.at[a], send_sem.at[h], recv_sem.at[h])
            gather(1, pprev, first_prev, a)
    part_prev[...] = gathered_sum()
    send(part_prev, got_own, s_part.at[1], r_part.at[1], (me_b, prv))

    for d in range(1, n_far):
        peer = lax.rem(far + d, n_far)
        arrived(chg_in3.at[peer], s_c3.at[d], r_c3.at[peer])
    charge = chg2[...]
    for d in range(1, n_far):
        charge = charge + chg_in3[lax.rem(far + d, n_far)]
    chg3[...] = charge
    for d in range(1, n_band):
        send(chg3, chg_in1.at[me_b], s_c1.at[d], r_c1.at[me_b], band_peer(d))

    loads[5].wait()
    for side in range(2):
        arrived(hhalo.at[side], s_hh.at[side], r_hh.at[side])
        arrived(rhalo.at[side], s_rh.at[side], r_rh.at[side])

    def around(cell):
        return (
            pltpu.roll(cell, 1, 0)
            + pltpu.roll(cell, rows - 1, 0)
            + pltpu.roll(cell, 1, 1)
            + pltpu.roll(cell, cols - 1, 1)
        )

    def start_plane(p):
        if p < 0:
            return hhalo[0, p + 2]
        if p >= planes:
            return hhalo[1, p - planes]
        return har_ref[p]

    def rho_plane(p):
        if p < 0:
            return rhalo[0]
        if p >= planes:
            return rhalo[1]
        return rho[p]

    inverse = 1.0 / (6.0 + SCREENING)
    for p in range(-1, planes + 1):
        total = start_plane(p - 1) + start_plane(p + 1) + around(start_plane(p))
        hone[p + 1] = (total + FOUR_PI * rho_plane(p)) * inverse
    for p in range(planes):
        total = hone[p] + hone[p + 2] + around(hone[p + 1])
        second = (total + FOUR_PI * rho[p]) * inverse
        root = jnp.exp(jnp.log(rho[p] * (3.0 / math.pi)) * (1.0 / 3.0))
        pre_ref[p] = second - root

    for part, mine, other, first in (
        (1, part_prev, got_prev, first_prev),
        (0, part_own, got_own, first_own),
    ):
        arrived(other, s_part.at[1 - part], r_part.at[1 - part])
        weighted = lax.dot_general(
            couple[...],
            mine[...] + other[...],
            (((1,), (1,)), ((), ())),
            precision=lax.Precision.HIGHEST,
            preferred_element_type=F32,
        ).astype(BF16)
        weights[part] = jnp.dot(weighted, belongs, preferred_element_type=F32)
        for a in range(atoms):
            n = part * atoms + a
            keep = step == lax.rem(box_ref[0, first + a], planes) - part * planes
            rows_a = weights[part, a * nproj : (a + 1) * nproj, :].reshape(nproj, 1, wide)
            placed = jnp.where(keep[None], rows_a, 0.0)
            placed = placed.reshape(nproj * width, wide).astype(BF16)
            term = jnp.dot(turned[n], placed, preferred_element_type=F32).astype(BF16)
            for y in range(rows):
                added[y, n * SLOT : (n + 1) * SLOT, :] = term[y * SLOT : (y + 1) * SLOT, :]
    for y in range(rows):
        fields[pl.ds(y, wide, stride=rows), :] = lax.dot_general(
            added[y], scat[...], (((0,), (0,)), ((), ())), preferred_element_type=F32
        )

    for d in range(1, n_band):
        peer = lax.rem(me_b + d, n_band)
        arrived(chg_in1.at[peer], s_c1.at[d], r_c1.at[peer])
    charge = chg3[...]
    for d in range(1, n_band):
        charge = charge + chg_in1[lax.rem(me_b + d, n_band)]
    charge_out[...] = charge
    for side in range(2):
        arrived(halo.at[side], s_halo.at[side], r_halo.at[side])
    for copy in sent:
        copy.wait_send()


def finish_terms(
    n_space,
    local_part,
    nonlocal_part,
    halo,
    charge_ref,
    pre_ref,
    ion_hbm,
    app_hbm,
    pot_hbm,
    app_ref,
    ion_ref,
    pot_ref,
    s_app,
    s_pot,
):
    orbs, planes, rows, cols = app_ref.shape
    cells = planes * rows
    batches = s_app.shape[0]
    some = orbs // batches
    scale = -0.5 / 12.0
    load = pltpu.make_async_copy(ion_hbm, ion_ref, s_pot.at[0])
    load.start()
    outs = []
    for n in range(batches):
        if n == batches // 2:
            inverse = 1.0 / (6.0 + SCREENING)
            total = jnp.sum(charge_ref[...], axis=(0, 1), keepdims=True)
            mean = total * (1.0 / (cells * cols * n_space))
            lift = FOUR_PI * inverse * (1.0 + 6.0 * inverse) * mean
            load.wait()
            for p in range(planes):
                pot_ref[p] = ion_ref[p] + (pre_ref[p] - lift)
            outs.append(pltpu.make_async_copy(pot_ref, pot_hbm, s_pot.at[1]))
            outs[-1].start()
        for o in range(n * some, (n + 1) * some):
            near_low, far_low = halo[0, o, 1].astype(F32), halo[0, o, 0].astype(F32)
            near_up, far_up = halo[1, o, 0].astype(F32), halo[1, o, 1].astype(F32)
            edge = {
                0: scale * (16.0 * near_low - far_low),
                1: (-scale) * near_low,
                planes - 2: (-scale) * near_up,
                planes - 1: scale * (16.0 * near_up - far_up),
            }
            for i in range(planes):
                at = o * cells + i * rows
                total = local_part[o, i * rows : (i + 1) * rows, :]
                total = total + nonlocal_part[at : at + rows, :]
                if i in edge:
                    total = total + edge[i]
                app_ref[o, i] = total.astype(BF16)
        at = pl.ds(n * some, some)
        outs.append(pltpu.make_async_copy(app_ref.at[at], app_hbm.at[at], s_app.at[n]))
        outs[-1].start()
    for copy in outs:
        copy.wait()


def local(
    n_band,
    n_space,
    orbitals,
    occupations,
    potential_in,
    ionic_potential,
    hartree_prev,
    projectors,
    box_start,
    coupling,
):
    orbs, planes, rows, cols = orbitals.shape
    atoms, nproj, width, square = projectors.shape
    cells = planes * rows
    wide = orbs * planes
    group = 8 if n_space % 8 == 0 else 2
    n_far = n_space // group
    share = atoms // n_band
    left, right = stencil_matrices(planes, rows, cols)
    left, right = jnp.asarray(left, BF16), jnp.asarray(right, BF16)
    vmem = pl.BlockSpec(memory_space=pltpu.VMEM)
    smem = pl.BlockSpec(memory_space=pltpu.SMEM)
    anywhere = pl.BlockSpec(memory_space=pl.ANY)
    dma = pltpu.SemaphoreType.DMA
    grid_f32 = jax.ShapeDtypeStruct(potential_in.shape, F32)
    halo_shape = (2, orbs, 2, rows, cols)
    turned_shape = (2 * atoms, square, nproj * width)
    scratch = [
        pltpu.VMEM(orbitals.shape, BF16),
        pltpu.VMEM(potential_in.shape, F32),
        pltpu.VMEM(hartree_prev.shape, F32),
        pltpu.VMEM(projectors.shape, BF16),
        pltpu.VMEM(left.shape, BF16),
        pltpu.VMEM(right.shape, BF16),
        pltpu.VMEM(projectors.shape, BF16),
        pltpu.VMEM((2, 2, rows, cols), F32),
        pltpu.VMEM((2, rows, cols), F32),
        pltpu.VMEM((planes, rows, cols), F32),
        pltpu.VMEM((planes, rows, cols), BF16),
        pltpu.VMEM((n_band, planes, rows, cols), BF16),
        pltpu.VMEM((planes, rows, cols), F32),
        pltpu.VMEM((ROWGROUP, cols), F32),
        pltpu.VMEM((ROWGROUP, cols), F32),
        pltpu.VMEM((ROWGROUP, cols), F32),
        pltpu.VMEM((n_band, ROWGROUP, cols), F32),
        pltpu.VMEM((group, ROWGROUP, cols), F32),
        pltpu.VMEM((n_far, ROWGROUP, cols), F32),
        pltpu.VMEM((2 * atoms * SLOT, cols), BF16),
        pltpu.VMEM((2 * atoms, square, wide), BF16),
        pltpu.VMEM(turned_shape, BF16),
        pltpu.VMEM((wide // cols, atoms * nproj * ROWGROUP, cols), F32),
        pltpu.VMEM((2, cols, wide), F32),
        pltpu.VMEM((rows, 2 * atoms * SLOT, wide), BF16),
        pltpu.VMEM((orbs, cols), F32),
        pltpu.VMEM((orbs, cols), F32),
        pltpu.VMEM((orbs, cols), F32),
        pltpu.VMEM((orbs, cols), F32),
        pltpu.VMEM((cols, cols), F32),
        pltpu.VMEM((planes + 2, rows, cols), F32),
        dma((6,)),
        dma((share,)),
        dma((share,)),
        dma((share,)),
        dma((share,)),
        dma((share,)),
        dma((share,)),
        dma((share,)),
        dma((share,)),
        dma((2,)),
        dma((2,)),
        dma((2,)),
        dma((2,)),
        dma((n_band,)),
        dma((n_band,)),
        dma((n_band,)),
        dma((n_band,)),
        dma((group,)),
        dma((group,)),
        dma((n_far,)),
        dma((n_far,)),
        dma((2,)),
        dma((2,)),
        dma((2,)),
        dma((2,)),
    ]
    handed = pl.pallas_call(
        functools.partial(exchange, (n_band, n_space, group)),
        out_shape=(
            pltpu.VMEM((orbs, cells, cols), F32),
            pltpu.VMEM((orbs * cells, cols), F32),
            pltpu.VMEM(halo_shape, BF16),
            pltpu.VMEM((ROWGROUP, cols), F32),
            pltpu.VMEM(potential_in.shape, F32),
        ),
        in_specs=[smem, smem, vmem] + [anywhere] * 6,
        out_specs=(vmem,) * 5,
        scratch_shapes=scratch,
        compiler_params=pltpu.CompilerParams(
            collective_id=0, has_side_effects=True, vmem_limit_bytes=54 * 1024 * 1024
        ),
    )(
        box_start,
        occupations,
        coupling,
        orbitals,
        potential_in,
        hartree_prev,
        projectors,
        left,
        right,
    )
    handed = [pltpu.with_memory_space_constraint(array, pltpu.VMEM) for array in handed]
    return pl.pallas_call(
        functools.partial(finish_terms, n_space),
        out_shape=(jax.ShapeDtypeStruct(orbitals.shape, BF16), grid_f32),
        in_specs=[vmem] * 5 + [anywhere],
        out_specs=(anywhere, anywhere),
        scratch_shapes=[
            pltpu.VMEM(orbitals.shape, BF16),
            pltpu.VMEM(potential_in.shape, F32),
            pltpu.VMEM(potential_in.shape, F32),
            dma((6,)),
            dma((2,)),
        ],
        compiler_params=pltpu.CompilerParams(vmem_limit_bytes=54 * 1024 * 1024),
    )(*handed, ionic_potential)


def solution(mesh):
    return jax.shard_map(
        functools.partial(local, mesh.shape["band"], mesh.shape["space"]),
        mesh=mesh,
        in_specs=(
            P("band", "space", None, None),
            P("band"),
            P("space", None, None),
            P("space", None, None),
            P("space", None, None),
            P("space", None, None, None),
            P(),
            P(),
        ),
        out_specs=(P("band", "space", None, None), P("space", None, None)),
        check_vma=False,
    )
```

```python
import functools
import math

import jax
import jax.numpy as jnp
import numpy as np
from jax import lax
from jax.experimental import pallas as pl
from jax.experimental.pallas import tpu as pltpu
from jax.sharding import PartitionSpec as P

SCREENING = 0.25
SWEEPS = 2
FOUR_PI = 4.0 * math.pi
ROWGROUP = 8
MESH = pl.DeviceIdType.MESH
F32 = jnp.float32
BF16 = jnp.bfloat16
SLOT = 16


def stencil_matrices(planes, rows, cols):
    def line(count, periodic):
        matrix = np.zeros((count, count), np.float32)
        for distance, weight in ((1, 16.0), (2, -1.0)):
            for sign in (-1, 1):
                for index in range(count):
                    other = index + sign * distance
                    if periodic:
                        other %= count
                    if 0 <= other < count:
                        matrix[index, other] += weight
        return matrix

    left = np.kron(line(planes, False), np.eye(rows)) + np.kron(np.eye(planes), line(rows, True))
    right = np.kron(np.eye(2), line(cols, True) - 90.0 * np.eye(cols))
    return left.astype(np.float32), right.astype(np.float32)


def tables(box_ref, first_own, first_prev, scat, atoms, cols):
    for part, first in ((0, first_own), (1, first_prev)):
        for a in range(atoms):
            want = lax.broadcasted_iota(jnp.int32, (SLOT, cols), 0) + box_ref[2, first + a]
            zcol = lax.broadcasted_iota(jnp.int32, (SLOT, cols), 1)
            at = (part * atoms + a) * SLOT
            scat[at : at + SLOT, :] = jnp.where(zcol == want, 1.0, 0.0).astype(BF16)


def ownership(orbs, wide, planes):
    lane = lax.broadcasted_iota(jnp.int32, (orbs, wide), 1) // planes
    own = lane == lax.broadcasted_iota(jnp.int32, (orbs, wide), 0)
    return jnp.where(own, 1.0, 0.0).astype(BF16)


def plane_steps(width, wide, planes):
    lane = lax.broadcasted_iota(jnp.int32, (width, wide), 1) % planes
    return lane - lax.broadcasted_iota(jnp.int32, (width, wide), 0)


def exchange(
    dims,
    box_ref,
    occ_ref,
    coup_ref,
    orb_hbm,
    vin_hbm,
    har_hbm,
    proj_hbm,
    left_hbm,
    right_hbm,
    local_part,
    fields,
    halo,
    charge_out,
    pre_ref,
    orb_ref,
    vin_ref,
    har_ref,
    proj_ref,
    left_ref,
    right_ref,
    pprev,
    relay,
    hhalo,
    rhalo,
    dens_f,
    dens_b,
    dens_in,
    rho,
    chg1,
    chg2,
    chg3,
    chg_in1,
    chg_in2,
    chg_in3,
    scat,
    gathered,
    turned,
    partial,
    weights,
    added,
    part_own,
    part_prev,
    got_own,
    got_prev,
    couple,
    hone,
    s_load,
    s_proj,
    r_proj,
    s_fwd,
    r_fwd,
    s_across,
    r_across,
    s_last,
    r_last,
    s_halo,
    r_halo,
    s_hh,
    r_hh,
    s_dens,
    r_dens,
    s_c1,
    r_c1,
    s_c2,
    r_c2,
    s_c3,
    r_c3,
    s_rh,
    r_rh,
    s_part,
    r_part,
    s_relay,
    r_relay,
):
    n_band, n_space, group = dims
    orbs, planes, rows, cols = orb_ref.shape
    atoms, nproj, width, square = proj_ref.shape
    cells = planes * rows
    wide = orbs * planes
    n_far = n_space // group
    share = atoms // n_band

    me_b = lax.axis_index("band")
    me_s = lax.axis_index("space")
    nxt = lax.rem(me_s + 1, n_space)
    prv = lax.rem(me_s + n_space - 1, n_space)
    core = lax.rem(me_b, 2)
    sib = me_b + 1 - 2 * core
    across = lax.rem(me_b + 2, n_band)
    beyond = lax.rem(sib + 2, n_band)
    near = me_s // n_far
    far = lax.rem(me_s, n_far)

    def band_peer(d):
        return (lax.rem(me_b + d, n_band), me_s)

    def near_peer(d):
        return (me_b, lax.rem(near + d, group) * n_far + far)

    def far_peer(d):
        return (me_b, near * n_far + lax.rem(far + d, n_far))

    partners = [(me_b, nxt), (me_b, prv)]
    partners += [band_peer(d) for d in range(1, n_band)]
    partners += [near_peer(d) for d in range(1, group)]
    partners += [far_peer(d) for d in range(1, n_far)]
    barrier = pltpu.get_barrier_semaphore()
    for partner in partners:
        pl.semaphore_signal(barrier, inc=1, device_id=partner, device_id_type=MESH)

    loads = []
    for n, (src, dst) in enumerate(
        (
            (orb_hbm, orb_ref),
            (proj_hbm, proj_ref),
            (left_hbm, left_ref),
            (right_hbm, right_ref),
            (vin_hbm, vin_ref),
            (har_hbm, har_ref),
        )
    ):
        loads.append(pltpu.make_async_copy(src, dst, s_load.at[n]))
        loads[n].start()

    pl.semaphore_wait(barrier, len(partners))

    sent = []

    def send(src, dst, send_sem, recv_sem, device):
        copy = pltpu.make_async_remote_copy(
            src_ref=src,
            dst_ref=dst,
            send_sem=send_sem,
            recv_sem=recv_sem,
            device_id=device,
            device_id_type=MESH,
        )
        copy.start()
        sent.append(copy)

    def arrived(dst, send_sem, recv_sem):
        pltpu.make_async_remote_copy(
            src_ref=dst,
            dst_ref=dst,
            send_sem=send_sem,
            recv_sem=recv_sem,
            device_id=(me_b, nxt),
            device_id_type=MESH,
        ).wait_recv()

    def send_projectors(h):
        a = me_b * share + h
        send(proj_hbm.at[a], pprev.at[a], s_proj.at[h], r_proj.at[h], (me_b, nxt))

    send_projectors(0)
    send(har_hbm.at[pl.ds(0, 2)], hhalo.at[1], s_hh.at[1], r_hh.at[1], (me_b, prv))
    send(har_hbm.at[pl.ds(planes - 2, 2)], hhalo.at[0], s_hh.at[0], r_hh.at[0], (me_b, nxt))
    first_own = me_s * atoms
    first_prev = prv * atoms
    tables(box_ref, first_own, first_prev, scat, atoms, cols)

    loads[0].wait()

    def density_plane(i, charge):
        total = jnp.zeros((rows, cols), F32)
        for o in range(orbs):
            field = orb_ref[o, i].astype(F32)
            at = (o * planes + i) * rows
            fields[pl.ds(pl.multiple_of(at, rows), rows), :] = field
            total = total + (occ_ref[o] * field) * field
        dens_f[i] = total
        dens_b[i] = total.astype(BF16)
        for r in range(0, rows, ROWGROUP):
            charge = charge + total[r : r + ROWGROUP]
        return charge

    chg1[...] = lax.fori_loop(0, planes, density_plane, jnp.zeros((ROWGROUP, cols), F32))
    for d in range(1, group):
        send(chg1, chg_in2.at[near], s_c2.at[d], r_c2.at[near], near_peer(d))
    for h in range(1, share):
        send_projectors(h)
    for d in range(1, n_band):
        send(dens_b, dens_in.at[me_b], s_dens.at[d], r_dens.at[me_b], band_peer(d))

    for y in range(rows):
        line = fields[pl.ds(y, wide, stride=rows), :].astype(BF16)
        cut = lax.dot_general(
            scat[...], line, (((1,), (1,)), ((), ())), preferred_element_type=F32
        ).astype(BF16)
        for n in range(2 * atoms):
            gathered[n, y * SLOT : (y + 1) * SLOT, :] = cut[n * SLOT : (n + 1) * SLOT, :]

    belongs = ownership(orbs, wide, planes)
    step = plane_steps(width, wide, planes)

    def gather(part, source, first, a):
        beta = source[a].reshape(nproj * width, square)
        turned[part * atoms + a] = beta.T
        pairs = jnp.dot(beta, gathered[part * atoms + a], preferred_element_type=F32)
        keep = step == lax.rem(box_ref[0, first + a], planes) - part * planes
        pairs = jnp.where(keep[None], pairs.reshape(nproj, width, wide), 0.0)
        folded = pairs[:, :ROWGROUP] + pairs[:, ROWGROUP:]
        folded = folded.reshape(nproj * ROWGROUP, wide)
        at = pl.ds(pl.multiple_of(a * nproj * ROWGROUP, ROWGROUP), nproj * ROWGROUP)
        for t in range(wide // cols):
            partial[t, at, :] = folded[:, t * cols : (t + 1) * cols]

    def gathered_sum():
        count = atoms * nproj
        tiles = []
        for t in range(wide // cols):
            total = partial[t, pl.ds(0, count, stride=ROWGROUP), :]
            for r in range(1, ROWGROUP):
                total = total + partial[t, pl.ds(r, count, stride=ROWGROUP), :]
            tiles.append(total)
        total = jnp.concatenate(tiles, axis=1)
        total = jnp.concatenate([total, jnp.zeros((cols - count, wide), F32)], axis=0)
        high = total.astype(BF16)
        low = (total - high.astype(F32)).astype(BF16)
        lanes = (((1,), (1,)), ((), ()))
        return lax.dot_general(
            belongs, high, lanes, preferred_element_type=F32
        ) + lax.dot_general(belongs, low, lanes, preferred_element_type=F32)

    def hand_on(h):
        a = me_b * share + h
        arrived(pprev.at[a], s_proj.at[h], r_proj.at[h])
        send(pprev.at[a], pprev.at[a], s_across.at[h], r_across.at[h], (across, me_s))
        send(pprev.at[a], pprev.at[a], s_fwd.at[h], r_fwd.at[h], (sib, me_s))

    def hand_across(h):
        a = across * share + h
        arrived(pprev.at[a], s_across.at[h], r_across.at[h])
        send(pprev.at[a], pprev.at[a], s_last.at[h], r_last.at[h], (sib, me_s))

    hand_on(0)
    loads[1].wait()
    for a in range(atoms):
        gather(0, proj_ref, first_own, a)
    part_own[...] = gathered_sum()
    send(part_own, got_prev, s_part.at[0], r_part.at[0], (me_b, nxt))

    hand_on(1)

    row_id = lax.broadcasted_iota(jnp.int32, (cols, nproj), 0) % nproj
    pick = jnp.where(
        row_id == lax.broadcasted_iota(jnp.int32, (cols, nproj), 1), 1.0, 0.0
    ).astype(F32)
    tall = jnp.dot(
        pick, coup_ref[...], precision=lax.Precision.HIGHEST, preferred_element_type=F32
    )
    full = lax.dot_general(
        tall,
        pick,
        (((1,), (1,)), ((), ())),
        precision=lax.Precision.HIGHEST,
        preferred_element_type=F32,
    )
    same = (
        lax.broadcasted_iota(jnp.int32, (cols, cols), 0) // nproj
        == lax.broadcasted_iota(jnp.int32, (cols, cols), 1) // nproj
    )
    couple[...] = jnp.where(same, full, 0.0)

    for d in range(1, group):
        peer = lax.rem(near + d, group)
        arrived(chg_in2.at[peer], s_c2.at[d], r_c2.at[peer])
    charge = chg1[...]
    for d in range(1, group):
        charge = charge + chg_in2[lax.rem(near + d, group)]
    chg2[...] = charge
    for d in range(1, n_far):
        send(chg2, chg_in3.at[far], s_c3.at[d], r_c3.at[far], far_peer(d))
    at_end = jnp.logical_and(far == n_far - 1, lax.rem(near, 4) == 2)
    on_way = jnp.logical_and(far == n_far - 1, lax.rem(near, 4) == 3)

    def planes_up(src, dst, send_sem, recv_sem, device):
        return pltpu.make_async_remote_copy(
            src_ref=src,
            dst_ref=dst,
            send_sem=send_sem,
            recv_sem=recv_sem,
            device_id=device,
            device_id_type=MESH,
        )

    upper = orb_ref.at[:, pl.ds(planes - 2, 2)]
    straight = planes_up(upper, halo.at[0], s_halo.at[0], r_halo.at[0], (me_b, nxt))
    turning = planes_up(upper, relay, s_halo.at[0], r_relay, near_peer(1))
    onward = planes_up(relay, halo.at[0], s_relay, r_halo.at[0], far_peer(1))
    pl.when(jnp.logical_not(at_end))(straight.start)
    pl.when(at_end)(turning.start)


    for h in range(share):
        gather(1, pprev, first_prev, me_b * share + h)

    for n in range(2, 5):
        loads[n].wait()
    for pair in range(orbs // 2):
        if pair == orbs // 4:
            hand_across(0)
        first, second = orb_ref[2 * pair], orb_ref[2 * pair + 1]
        both = jnp.concatenate([first.reshape(cells, cols), second.reshape(cells, cols)], axis=1)
        lap = jnp.dot(left_ref[...], both, preferred_element_type=F32)
        lap = lap + jnp.dot(both, right_ref[...], preferred_element_type=F32)
        vin = vin_ref[...].reshape(cells, cols)
        for n in range(2):
            field = both[:, n * cols : (n + 1) * cols].astype(F32)
            local_part[2 * pair + n] = lap[:, n * cols : (n + 1) * cols] * (-0.5 / 12.0) + vin * field
    send(orb_ref.at[:, pl.ds(0, 2)], halo.at[1], s_halo.at[1], r_halo.at[1], (me_b, prv))
    hand_across(1)
    for h in range(share):
        gather(1, pprev, first_prev, across * share + h)

    @pl.when(on_way)
    def _():
        turning.wait_recv()
        onward.start()

    for d in range(1, n_band):
        peer = lax.rem(me_b + d, n_band)
        arrived(dens_in.at[peer], s_dens.at[d], r_dens.at[peer])
    total_density = dens_f[...]
    for d in range(1, n_band):
        total_density = total_density + dens_in[lax.rem(me_b + d, n_band)].astype(F32)
    rho[...] = total_density
    send(rho.at[0], rhalo.at[1], s_rh.at[1], r_rh.at[1], (me_b, prv))
    send(rho.at[planes - 1], rhalo.at[0], s_rh.at[0], r_rh.at[0], (me_b, nxt))
    for base, send_sem, recv_sem in ((sib, s_fwd, r_fwd), (beyond, s_last, r_last)):
        for h in range(share):
            a = base * share + h
            arrived(pprev.at[a], send_sem.at[h], recv_sem.at[h])
            gather(1, pprev, first_prev, a)
    part_prev[...] = gathered_sum()
    send(part_prev, got_own, s_part.at[1], r_part.at[1], (me_b, prv))

    for d in range(1, n_far):
        peer = lax.rem(far + d, n_far)
        arrived(chg_in3.at[peer], s_c3.at[d], r_c3.at[peer])
    charge = chg2[...]
    for d in range(1, n_far):
        charge = charge + chg_in3[lax.rem(far + d, n_far)]
    chg3[...] = charge
    for d in range(1, n_band):
        send(chg3, chg_in1.at[me_b], s_c1.at[d], r_c1.at[me_b], band_peer(d))

    loads[5].wait()
    for side in range(2):
        arrived(hhalo.at[side], s_hh.at[side], r_hh.at[side])
        arrived(rhalo.at[side], s_rh.at[side], r_rh.at[side])

    def around(cell):
        return (
            pltpu.roll(cell, 1, 0)
            + pltpu.roll(cell, rows - 1, 0)
            + pltpu.roll(cell, 1, 1)
            + pltpu.roll(cell, cols - 1, 1)
        )

    def start_plane(p):
        if p < 0:
            return hhalo[0, p + 2]
        if p >= planes:
            return hhalo[1, p - planes]
        return har_ref[p]

    def rho_plane(p):
        if p < 0:
            return rhalo[0]
        if p >= planes:
            return rhalo[1]
        return rho[p]

    inverse = 1.0 / (6.0 + SCREENING)
    for p in range(-1, planes + 1):
        total = start_plane(p - 1) + start_plane(p + 1) + around(start_plane(p))
        hone[p + 1] = (total + FOUR_PI * rho_plane(p)) * inverse
    for p in range(planes):
        total = hone[p] + hone[p + 2] + around(hone[p + 1])
        second = (total + FOUR_PI * rho[p]) * inverse
        root = jnp.exp(jnp.log(rho[p] * (3.0 / math.pi)) * (1.0 / 3.0))
        pre_ref[p] = second - root

    for part, mine, other, first in (
        (1, part_prev, got_prev, first_prev),
        (0, part_own, got_own, first_own),
    ):
        arrived(other, s_part.at[1 - part], r_part.at[1 - part])
        weighted = lax.dot_general(
            couple[...],
            mine[...] + other[...],
            (((1,), (1,)), ((), ())),
            precision=lax.Precision.HIGHEST,
            preferred_element_type=F32,
        ).astype(BF16)
        weights[part] = jnp.dot(weighted, belongs, preferred_element_type=F32)
        for a in range(atoms):
            n = part * atoms + a
            keep = step == lax.rem(box_ref[0, first + a], planes) - part * planes
            rows_a = weights[part, a * nproj : (a + 1) * nproj, :].reshape(nproj, 1, wide)
            placed = jnp.where(keep[None], rows_a, 0.0)
            placed = placed.reshape(nproj * width, wide).astype(BF16)
            term = jnp.dot(turned[n], placed, preferred_element_type=F32).astype(BF16)
            for y in range(rows):
                added[y, n * SLOT : (n + 1) * SLOT, :] = term[y * SLOT : (y + 1) * SLOT, :]
    for y in range(rows):
        fields[pl.ds(y, wide, stride=rows), :] = lax.dot_general(
            added[y], scat[...], (((0,), (0,)), ((), ())), preferred_element_type=F32
        )

    for d in range(1, n_band):
        peer = lax.rem(me_b + d, n_band)
        arrived(chg_in1.at[peer], s_c1.at[d], r_c1.at[peer])
    charge = chg3[...]
    for d in range(1, n_band):
        charge = charge + chg_in1[lax.rem(me_b + d, n_band)]
    charge_out[...] = charge
    for side in range(2):
        arrived(halo.at[side], s_halo.at[side], r_halo.at[side])
    for copy in sent:
        copy.wait_send()
    straight.wait_send()
    pl.when(on_way)(onward.wait_send)


def finish_terms(
    n_space,
    local_part,
    nonlocal_part,
    halo,
    charge_ref,
    pre_ref,
    ion_hbm,
    app_hbm,
    pot_hbm,
    app_ref,
    ion_ref,
    pot_ref,
    s_app,
    s_pot,
):
    orbs, planes, rows, cols = app_ref.shape
    cells = planes * rows
    batches = s_app.shape[0]
    some = orbs // batches
    scale = -0.5 / 12.0
    load = pltpu.make_async_copy(ion_hbm, ion_ref, s_pot.at[0])
    load.start()
    outs = []
    for n in range(batches):
        if n == batches // 2:
            inverse = 1.0 / (6.0 + SCREENING)
            total = jnp.sum(charge_ref[...], axis=(0, 1), keepdims=True)
            mean = total * (1.0 / (cells * cols * n_space))
            lift = FOUR_PI * inverse * (1.0 + 6.0 * inverse) * mean
            load.wait()
            for p in range(planes):
                pot_ref[p] = ion_ref[p] + (pre_ref[p] - lift)
            outs.append(pltpu.make_async_copy(pot_ref, pot_hbm, s_pot.at[1]))
            outs[-1].start()
        for o in range(n * some, (n + 1) * some):
            near_low, far_low = halo[0, o, 1].astype(F32), halo[0, o, 0].astype(F32)
            near_up, far_up = halo[1, o, 0].astype(F32), halo[1, o, 1].astype(F32)
            edge = {
                0: scale * (16.0 * near_low - far_low),
                1: (-scale) * near_low,
                planes - 2: (-scale) * near_up,
                planes - 1: scale * (16.0 * near_up - far_up),
            }
            for i in range(planes):
                at = o * cells + i * rows
                total = local_part[o, i * rows : (i + 1) * rows, :]
                total = total + nonlocal_part[at : at + rows, :]
                if i in edge:
                    total = total + edge[i]
                app_ref[o, i] = total.astype(BF16)
        at = pl.ds(n * some, some)
        outs.append(pltpu.make_async_copy(app_ref.at[at], app_hbm.at[at], s_app.at[n]))
        outs[-1].start()
    for copy in outs:
        copy.wait()


def local(
    n_band,
    n_space,
    orbitals,
    occupations,
    potential_in,
    ionic_potential,
    hartree_prev,
    projectors,
    box_start,
    coupling,
):
    orbs, planes, rows, cols = orbitals.shape
    atoms, nproj, width, square = projectors.shape
    cells = planes * rows
    wide = orbs * planes
    group = 8 if n_space % 8 == 0 else 2
    n_far = n_space // group
    share = atoms // n_band
    left, right = stencil_matrices(planes, rows, cols)
    left, right = jnp.asarray(left, BF16), jnp.asarray(right, BF16)
    vmem = pl.BlockSpec(memory_space=pltpu.VMEM)
    smem = pl.BlockSpec(memory_space=pltpu.SMEM)
    anywhere = pl.BlockSpec(memory_space=pl.ANY)
    dma = pltpu.SemaphoreType.DMA
    grid_f32 = jax.ShapeDtypeStruct(potential_in.shape, F32)
    halo_shape = (2, orbs, 2, rows, cols)
    turned_shape = (2 * atoms, square, nproj * width)
    scratch = [
        pltpu.VMEM(orbitals.shape, BF16),
        pltpu.VMEM(potential_in.shape, F32),
        pltpu.VMEM(hartree_prev.shape, F32),
        pltpu.VMEM(projectors.shape, BF16),
        pltpu.VMEM(left.shape, BF16),
        pltpu.VMEM(right.shape, BF16),
        pltpu.VMEM(projectors.shape, BF16),
        pltpu.VMEM(halo_shape[1:], BF16),
        pltpu.VMEM((2, 2, rows, cols), F32),
        pltpu.VMEM((2, rows, cols), F32),
        pltpu.VMEM((planes, rows, cols), F32),
        pltpu.VMEM((planes, rows, cols), BF16),
        pltpu.VMEM((n_band, planes, rows, cols), BF16),
        pltpu.VMEM((planes, rows, cols), F32),
        pltpu.VMEM((ROWGROUP, cols), F32),
        pltpu.VMEM((ROWGROUP, cols), F32),
        pltpu.VMEM((ROWGROUP, cols), F32),
        pltpu.VMEM((n_band, ROWGROUP, cols), F32),
        pltpu.VMEM((group, ROWGROUP, cols), F32),
        pltpu.VMEM((n_far, ROWGROUP, cols), F32),
        pltpu.VMEM((2 * atoms * SLOT, cols), BF16),
        pltpu.VMEM((2 * atoms, square, wide), BF16),
        pltpu.VMEM(turned_shape, BF16),
        pltpu.VMEM((wide // cols, atoms * nproj * ROWGROUP, cols), F32),
        pltpu.VMEM((2, cols, wide), F32),
        pltpu.VMEM((rows, 2 * atoms * SLOT, wide), BF16),
        pltpu.VMEM((orbs, cols), F32),
        pltpu.VMEM((orbs, cols), F32),
        pltpu.VMEM((orbs, cols), F32),
        pltpu.VMEM((orbs, cols), F32),
        pltpu.VMEM((cols, cols), F32),
        pltpu.VMEM((planes + 2, rows, cols), F32),
        dma((6,)),
        dma((share,)),
        dma((share,)),
        dma((share,)),
        dma((share,)),
        dma((share,)),
        dma((share,)),
        dma((share,)),
        dma((share,)),
        dma((2,)),
        dma((2,)),
        dma((2,)),
        dma((2,)),
        dma((n_band,)),
        dma((n_band,)),
        dma((n_band,)),
        dma((n_band,)),
        dma((group,)),
        dma((group,)),
        dma((n_far,)),
        dma((n_far,)),
        dma((2,)),
        dma((2,)),
        dma((2,)),
        dma((2,)),
        dma,
        dma,
    ]
    handed = pl.pallas_call(
        functools.partial(exchange, (n_band, n_space, group)),
        out_shape=(
            pltpu.VMEM((orbs, cells, cols), F32),
            pltpu.VMEM((orbs * cells, cols), F32),
            pltpu.VMEM(halo_shape, BF16),
            pltpu.VMEM((ROWGROUP, cols), F32),
            pltpu.VMEM(potential_in.shape, F32),
        ),
        in_specs=[smem, smem, vmem] + [anywhere] * 6,
        out_specs=(vmem,) * 5,
        scratch_shapes=scratch,
        compiler_params=pltpu.CompilerParams(
            collective_id=0, has_side_effects=True, vmem_limit_bytes=54 * 1024 * 1024
        ),
    )(
        box_start,
        occupations,
        coupling,
        orbitals,
        potential_in,
        hartree_prev,
        projectors,
        left,
        right,
    )
    handed = [pltpu.with_memory_space_constraint(array, pltpu.VMEM) for array in handed]
    return pl.pallas_call(
        functools.partial(finish_terms, n_space),
        out_shape=(jax.ShapeDtypeStruct(orbitals.shape, BF16), grid_f32),
        in_specs=[vmem] * 5 + [anywhere],
        out_specs=(anywhere, anywhere),
        scratch_shapes=[
            pltpu.VMEM(orbitals.shape, BF16),
            pltpu.VMEM(potential_in.shape, F32),
            pltpu.VMEM(potential_in.shape, F32),
            dma((6,)),
            dma((2,)),
        ],
        compiler_params=pltpu.CompilerParams(vmem_limit_bytes=54 * 1024 * 1024),
    )(*handed, ionic_potential)


def solution(mesh):
    return jax.shard_map(
        functools.partial(local, mesh.shape["band"], mesh.shape["space"]),
        mesh=mesh,
        in_specs=(
            P("band", "space", None, None),
            P("band"),
            P("space", None, None),
            P("space", None, None),
            P("space", None, None),
            P("space", None, None, None),
            P(),
            P(),
        ),
        out_specs=(P("band", "space", None, None), P("space", None, None)),
        check_vma=False,
    )
```
